128 devices in a mesh: slab: 32 (over z, x, core), face: 4 (over y).
Axes of the slice: x: 4, y: 4, z: 4, core: 2. Of those that a mesh axis runs over, the one named last changes fastest.
Arguments:
- displacement: float32 [6, 8192, 1024], P(None, 'slab', 'face'), may hold values from -6 to 6
- load: float32 [6, 8192, 1024], P(None, 'slab', 'face'), may hold values from -6 to 6
- stiffness: float32 [8192, 1024], P('slab', 'face'), may hold values from 0.02 to 0.5
- slave_row: int32 [16384], P(('slab', 'face')), may hold values from 0 to 255
- master_dev: int32 [16384, 1], P(('slab', 'face')), may hold values from 0 to 127; in each aligned block of 128 rows (0 to 127, 128 to 255, ...) at most 4 rows name the same one
- master_row: int32 [16384], P(('slab', 'face')), may hold values from 0 to 255
- seg_count: int32 [16384], P(('slab', 'face')), may hold values from 16 to 24
- quad_coords: float32 [16384, 4, 384], P(('slab', 'face')), may hold values from -0.98 to 0.98
- quad_weights: float32 [16384, 384], P(('slab', 'face')), may hold values from 0.002 to 0.02
Outputs:
- relaxed: float32 [6, 8192, 1024], P(None, 'slab', 'face')
- contact_gap: float32 [16384, 3, 256], P(('slab', 'face'))
The draws below stay inside these ranges and needn't reach their ends.
Inputs may be any that keep to these rules, and one draw needn't show every extreme that they name: `master_dev`: among the 128 pairs of one device no owner device is named more than 4 times, and in some device one owner is named exactly 4 times.
All inputs are finite; a program needn't handle non-finite values.
Results may differ from the reference program's by a relative error of at most 0.0003.
Values sent between devices are 32-bit elements; how exact they have to be, the bound alone decides.
No kernel may reach another device: no remote copies, remote signals or barrier semaphores. Data moves between devices by JAX's collectives and lax.ppermute only.
A program may use at most 128 MiB of HBM per device.

```python
import math
import jax
import jax.numpy as jnp
import numpy as np
from jax import lax

CS = 256
PAIR_DEV = 128
MODES = 16
NODES = 256
QPTS = 16
SEGS = 24
SEG_MIN = 16
KQ = 384
CAP = 4
SWEEPS = 2
PAIRS = 16384
NS = 8192
NF = 1024
N_SLAB = 32
N_FACE = 4


def set_ends(values, rng, least, largest):
    extent = values.shape
    spot = [jax.random.randint(jax.random.fold_in(rng, axis), (), 0, extent[axis]) for axis in range(len(extent))]
    values = values.at[tuple(spot)].set(least)
    longest = extent.index(max(extent))
    spot[longest] = (spot[longest] + 1) % extent[longest]
    return values.at[tuple(spot)].set(largest)


def block_scale(stream_key, shape, pieces, least, high):
    factor_of, own = 1.0, jax.random.fold_in(stream_key, 6)
    for position, parts in pieces:
        heights = jnp.exp(jax.random.uniform(jax.random.fold_in(own, position), (parts,), jnp.float32, least / len(pieces), high / len(pieces)))
        factor_of = factor_of * jnp.repeat(heights, shape[position] // parts).reshape([-1 if axis == position else 1 for axis in range(len(shape))])
    return factor_of


def deal_out(key, own, number, rows, amount, top, limit, skew):
    ranking = jax.random.permutation(key, amount)
    heavy_load, common = load_shares(amount, rows * top, limit, skew, True), load_shares(amount, rows * top, limit, skew, False)
    places = jnp.arange(amount)

    def named(lengths, rotation):
        used = int((lengths > 0).sum())
        fixed = max(1, used // 4)
        moved = fixed + (places - fixed + rotation * (used - fixed)) % max(1, amount - fixed)
        return jnp.zeros((amount,), jnp.int32).at[ranking[jnp.where(places < fixed, places, moved)]].set(jnp.asarray(lengths, jnp.int32))

    lengths = jnp.where(number % 4 == 0, named(heavy_load, number // 4), named(common, number - number // 4 - 1))
    mixed = jax.random.permutation(jax.random.fold_in(own, 3), amount)
    donor, sink = mixed[0:amount // 2 * 2:2], mixed[1:amount // 2 * 2:2]
    room = jnp.minimum(lengths[donor] - 1, limit - lengths[sink]) // 2
    room = jnp.where((donor == ranking[0]) | (sink == ranking[0]) | (lengths[sink] == 0), 0, jnp.maximum(room, 0))
    moved = jax.random.randint(jax.random.fold_in(own, 4), (amount // 2,), 0, 1 << 20) % (room + 1)
    lengths = lengths.at[donor].add(-moved).at[sink].add(moved)
    members = jnp.searchsorted(jnp.cumsum(lengths), jnp.arange(rows * top), side="right").astype(jnp.int32)
    table = members.reshape(top, rows).T
    table = table[jax.random.permutation(jax.random.fold_in(own, 1), rows)]
    rotation = jax.random.randint(jax.random.fold_in(own, 2), (rows, 1), 0, top)
    return jnp.take_along_axis(table, (jnp.arange(top)[None, :] + rotation) % top, axis=1)


def load_shares(count, total, limit, slope, full):
    loads = [(1 << 20) // math.isqrt(grade ** slope) + 1 for grade in range(1, count + 1)]
    largest = limit if full else min(limit, max(-(-total // count), total * loads[0] // sum(loads)))
    least = 1 if total - largest >= count - 1 else 0
    given, surplus = [largest] + [least] * (count - 1), total - largest - least * (count - 1)
    while surplus > 0:
        free = [i for i in range(1, count) if given[i] < largest] or [i for i in range(1, count) if given[i] < limit]
        mass, remaining = sum([loads[i] for i in free]), surplus
        for i in free:
            addition = min(limit - given[i], max(1, remaining * loads[i] // mass), surplus)
            given[i] = given[i] + addition
            surplus = surplus - addition
    return np.array(given)


def scatter_about(stream_key, shape, deviation, limit, split=(), held_as=jnp.bfloat16):
    values = deviation * jax.random.normal(stream_key, shape, jnp.float32)
    if split:
        values = values * block_scale(stream_key, shape, split, -0.22, 0.18)
    return jnp.clip(values, -limit, limit).astype(held_as)


def setup_inputs(seed: int = 0) -> dict:
    key_list = jax.random.split(jax.random.key(seed), 10)
    displacement = scatter_about(key_list[0], (6, NS, NF), 1.0, 6.0, ((1, 32), (2, 4)), jnp.float32)
    load = scatter_about(key_list[1], (6, NS, NF), 1.0, 6.0, ((1, 32), (2, 4)), jnp.float32)
    stiffness = jnp.clip(jnp.exp(math.log(0.5) - 3.218876 * jax.random.uniform(key_list[2], (NS, NF), jnp.float32) ** block_scale(key_list[2], (NS, NF), ((0, 32), (1, 4)), -0.2, 0.2)), 0.02, 0.5)
    slave_row = set_ends(jax.random.randint(key_list[3], (PAIRS,), 0, CS), jax.random.fold_in(key_list[3], 1), 0, CS - 1).astype(jnp.int32)
    master_dev_keys = jax.random.split(jax.random.fold_in(key_list[4], 1), PAIRS // PAIR_DEV)
    master_dev_turns = jax.random.permutation(jax.random.fold_in(key_list[4], 3), PAIRS // PAIR_DEV)
    master_dev = jax.vmap(lambda own, number: deal_out(jax.random.fold_in(key_list[4], 2), own, number, PAIR_DEV, N_SLAB * N_FACE, 1, CAP, 2))(master_dev_keys, master_dev_turns).reshape((PAIRS, 1))
    master_row = set_ends(jax.random.randint(key_list[5], (PAIRS,), 0, CS), jax.random.fold_in(key_list[5], 1), 0, CS - 1).astype(jnp.int32)
    seg_count = set_ends(jax.random.randint(key_list[6], (PAIRS,), SEG_MIN, SEGS + 1), jax.random.fold_in(key_list[6], 1), SEG_MIN, SEGS).astype(jnp.int32)
    quad_coords = jnp.clip(jax.random.uniform(key_list[7], (PAIRS, 4, KQ), jnp.float32, -0.98, 0.98) * block_scale(key_list[7], (PAIRS, 4, KQ), ((0, 128),), -0.4, 0.0), -0.98, 0.98)
    quad_weights = jnp.clip(jnp.exp(math.log(0.02) - 2.30258502 * jax.random.uniform(key_list[8], (PAIRS, KQ), jnp.float32) ** block_scale(key_list[8], (PAIRS, KQ), ((0, 128),), -0.2, 0.2)), 0.002, 0.02)
    return {"displacement": displacement, "load": load, "stiffness": stiffness, "slave_row": slave_row, "master_dev": master_dev, "master_row": master_row, "seg_count": seg_count, "quad_coords": quad_coords, "quad_weights": quad_weights}


PENALTY = 0.5
RELAX = 0.8


def mode_table(coord_s, coord_t, mode_count):
    degree = jnp.arange(mode_count).astype(coord_s.dtype)
    along_s = jnp.cos(degree[:, None] * jnp.arccos(coord_s)[..., None, :])
    across = jnp.cos(degree[:, None] * jnp.arccos(coord_t)[..., None, :])
    tensor = along_s[..., :, None, :] * across[..., None, :, :]
    return tensor.reshape(tensor.shape[:-3] + (mode_count * mode_count, tensor.shape[-1]))


def to_patches(field_in, devices):
    depth = field_in.shape[0]
    blocked = field_in.reshape(depth, N_SLAB, CS, N_FACE, NODES)
    return blocked.transpose(0, 1, 3, 2, 4).reshape(depth, devices * CS, NODES)


def from_patches(patches, devices):
    depth = patches.shape[0]
    blocked = patches.reshape(depth, N_SLAB, N_FACE, CS, NODES)
    return blocked.transpose(0, 1, 3, 2, 4).reshape(depth, N_SLAB * CS, N_FACE * NODES)


def pair_block(inputs):
    slave_u, master_u, coords, weights = inputs
    highest = lax.Precision.HIGHEST
    slave_tab = mode_table(coords[:, 0], coords[:, 1], MODES) * weights[:, None, :]
    slave_tab = lax.optimization_barrier(slave_tab.astype(jnp.bfloat16)).astype(jnp.float32)
    master_tab = mode_table(coords[:, 2], coords[:, 3], MODES)
    master_tab = lax.optimization_barrier(master_tab.astype(jnp.bfloat16)).astype(jnp.float32)
    projected = jnp.einsum('bcj,bjk->bck', master_u, master_tab, precision=highest)
    pulled = jnp.einsum('bck,bik->bci', projected, slave_tab, precision=highest)
    gap_block = slave_u - pulled
    pushed = jnp.einsum('bci,bik->bck', PENALTY * gap_block, slave_tab, precision=highest)
    pushed_back = jnp.einsum('bck,bjk->bcj', pushed, master_tab, precision=highest)
    return gap_block, pushed_back


def reference(displacement, load, stiffness, slave_row, master_dev, master_row, seg_count, quad_coords, quad_weights):
    devices = N_SLAB * N_FACE
    pair_count = slave_row.shape[0]
    patches = to_patches(displacement, devices)
    owner_dev = (jnp.arange(pair_count) // PAIR_DEV).astype(jnp.int32)
    slave_id = (owner_dev * CS + slave_row).astype(jnp.int32)
    master_id = (master_dev[:, 0] * CS + master_row).astype(jnp.int32)
    slave_u = jnp.take(patches[0:3], slave_id, axis=1).transpose(1, 0, 2)
    master_u = jnp.take(patches[3:6], master_id, axis=1).transpose(1, 0, 2)
    points = jnp.arange(KQ)
    active = points[None, :] < (seg_count * QPTS)[:, None]
    weights = jnp.where(active, quad_weights, 0.0)
    blocks = pair_count // PAIR_DEV

    def blocked(array):
        return array.reshape((blocks, PAIR_DEV) + array.shape[1:])

    gap_all, pushed_back = lax.map(pair_block, (blocked(slave_u), blocked(master_u), blocked(quad_coords), blocked(weights)))
    gap_all = gap_all.reshape(pair_count, 3, NODES)
    pushed_back = pushed_back.reshape(pair_count, 3, NODES)
    contact = jnp.zeros_like(patches)
    contact = contact.at[0:3, slave_id].add(-PENALTY * gap_all.transpose(1, 0, 2))
    contact = contact.at[3:6, master_id].add(pushed_back.transpose(1, 0, 2))
    right_side = load + from_patches(contact, devices)
    diagonal = 4.0 + stiffness
    current = displacement
    for sweep_index in range(SWEEPS):
        padded = jnp.pad(current, ((0, 0), (1, 1), (1, 1)))
        beside = padded[:, 2:, 1:-1] + padded[:, :-2, 1:-1] + padded[:, 1:-1, 2:] + padded[:, 1:-1, :-2]
        residual = right_side - (diagonal * current - beside)
        current = current + RELAX * residual / diagonal
    return current, gap_all
```

```python
import functools

import jax
import jax.numpy as jnp
from jax import lax
from jax.experimental import pallas as pl
from jax.experimental.pallas import tpu as pltpu
from jax.sharding import PartitionSpec as P

MODES = 16
QPTS = 16
CAP = 4
PENALTY = 0.5
RELAX = 0.8
DEVICES = 128
PAIRS = 128
NODES = 256
ROWS = 256
PARTS = 6
SLOT_ROWS = DEVICES * CAP * PARTS
PAIR_BLOCK = 8

f32 = jnp.float32
bf16 = jnp.bfloat16
AXES = ("slab", "face")


def vmem():
    return pl.BlockSpec(memory_space=pltpu.VMEM)


def smem():
    return pl.BlockSpec(memory_space=pltpu.SMEM)


def params():
    return pltpu.CompilerParams(vmem_limit_bytes=48 << 20)


def slots_kernel(dev_ref, row_ref, request_ref, slot_ref):
    dev = dev_ref[...]
    row = row_ref[...]
    spread = jnp.broadcast_to(dev, (PAIRS, PAIRS))
    across = jnp.transpose(spread)
    first = lax.broadcasted_iota(jnp.int32, (PAIRS, PAIRS), 0)
    second = lax.broadcasted_iota(jnp.int32, (PAIRS, PAIRS), 1)
    same = jnp.where((spread == across) & (first < second), 1.0, 0.0)
    rank = jnp.sum(same, axis=0, keepdims=True).astype(jnp.int32)
    slot_ref[...] = dev * CAP + rank
    hits = spread == first
    result = jnp.full((DEVICES, 128), -1, jnp.int32)
    for k in range(CAP):
        chosen = jnp.where(hits & (rank == k), (row + 1).astype(f32), 0.0)
        found = jnp.sum(chosen, axis=1, keepdims=True).astype(jnp.int32) - 1
        result = jnp.where(second == k, found, result)
    request_ref[...] = result.reshape(DEVICES, 1, 128)


def slots(dev, row):
    return pl.pallas_call(
        slots_kernel,
        out_shape=[
            jax.ShapeDtypeStruct((DEVICES, 1, 128), jnp.int32),
            jax.ShapeDtypeStruct((1, PAIRS), jnp.int32),
        ],
        in_specs=[vmem(), vmem()],
        out_specs=[vmem(), vmem()],
        name="slots",
    )(dev, row)


def serve_kernel(asked_ref, field_ref, out_ref):
    def one(s, carry):
        for k in range(CAP):
            r = jnp.maximum(asked_ref[s * 128 + k], 0)
            for c in range(3):
                line = field_ref[c, pl.ds(r, 1), :]
                out_ref[s, pl.ds(k * PARTS + c, 1), :] = line[:, 0:128]
                out_ref[s, pl.ds(k * PARTS + 3 + c, 1), :] = line[:, 128:256]
        return carry

    lax.fori_loop(0, DEVICES, one, 0, unroll=4)


def serve(asked, field):
    return pl.pallas_call(
        serve_kernel,
        grid=(1,),
        out_shape=jax.ShapeDtypeStruct((DEVICES, CAP * PARTS, 128), f32),
        in_specs=[smem(), pl.BlockSpec((3, ROWS, NODES), lambda i: (1, 0, 0))],
        out_specs=pl.BlockSpec((DEVICES, CAP * PARTS, 128), lambda i: (0, 0, 0)),
        compiler_params=params(),
        name="serve",
    )(asked, field)


def two_pieces(u):
    high = u.astype(bf16)
    low = u - high.astype(f32)
    return jnp.concatenate([high.astype(f32), low], axis=0).astype(bf16)


def times(pieces, table):
    both = lax.dot_general(pieces, table, (((1,), (0,)), ((), ())), preferred_element_type=f32)
    return both[0:8] + both[8:16]


def times_transposed(pieces, table):
    both = lax.dot_general(pieces, table, (((1,), (1,)), ((), ())), preferred_element_type=f32)
    return both[0:8] + both[8:16]


def mortar_kernel(
    slot_ref, row_ref, coords_ref, weights_ref, field_ref, load_ref, arrived_ref,
    gap_ref, outgoing_ref, right_ref, modes, slave_tab, master_tab,
):
    step = pl.program_id(0)

    @pl.when(step == 0)
    def _():
        outgoing_ref[...] = jnp.zeros_like(outgoing_ref)
        right_ref[...] = load_ref[...]

    for k in range(4):
        x = coords_ref[k]
        now = weights_ref[...] if k == 0 else jnp.ones_like(x)
        later = now * x
        twice = x + x
        for n in range(MODES):
            modes[k, :, n, :] = now
            now, later = later, twice * later - now
    for p in range(PAIR_BLOCK):
        for table, along, across in ((master_tab, 2, 3), (slave_tab, 0, 1)):
            inner = modes[across, p]
            for a in range(MODES):
                outer = modes[along, p, a : a + 1, :]
                table[p, a * MODES : (a + 1) * MODES, :] = (inner * outer).astype(bf16)
    rest = jnp.zeros((5, NODES), f32)
    master = []
    for p in range(PAIR_BLOCK):
        start = slot_ref[step * PAIR_BLOCK + p] * PARTS
        both = arrived_ref[pl.ds(start, PARTS), :]
        u = jnp.concatenate([both[0:3], both[3:6]], axis=1)
        master.append(two_pieces(jnp.concatenate([u, rest], axis=0)))
    projected = [two_pieces(times(master[p], master_tab[p])) for p in range(PAIR_BLOCK)]
    pulled = [times_transposed(projected[p], slave_tab[p]) for p in range(PAIR_BLOCK)]
    half_gaps = []
    for p in range(PAIR_BLOCK):
        r = row_ref[step * PAIR_BLOCK + p]
        lines = [field_ref[c, pl.ds(r, 1), :] for c in range(3)]
        gap = jnp.concatenate(lines + [rest], axis=0) - pulled[p]
        gap_ref[p] = gap[0:3]
        half = PENALTY * gap
        half_gaps.append(half)
    pushed = [two_pieces(times(two_pieces(half_gaps[p]), slave_tab[p])) for p in range(PAIR_BLOCK)]
    back = [times_transposed(pushed[p], master_tab[p]) for p in range(PAIR_BLOCK)]
    for p in range(PAIR_BLOCK):
        start = slot_ref[step * PAIR_BLOCK + p] * PARTS
        outgoing_ref[pl.ds(start, PARTS), :] = jnp.concatenate(
            [back[p][0:3, 0:128], back[p][0:3, 128:256]], axis=0
        )
        r = row_ref[step * PAIR_BLOCK + p]
        for c in range(3):
            right_ref[c, pl.ds(r, 1), :] = right_ref[c, pl.ds(r, 1), :] - half_gaps[p][c : c + 1]


def mortar(slot, slave_row, coords, weights, field, load, arrived):
    points = weights.shape[1]
    whole = lambda i, *_: (0, 0, 0)
    return pl.pallas_call(
        mortar_kernel,
        grid_spec=pltpu.PrefetchScalarGridSpec(
            num_scalar_prefetch=2,
            grid=(PAIRS // PAIR_BLOCK,),
            in_specs=[
                pl.BlockSpec((4, PAIR_BLOCK, points), lambda i, *_: (0, i, 0)),
                pl.BlockSpec((PAIR_BLOCK, points), lambda i, *_: (i, 0)),
                pl.BlockSpec((3, ROWS, NODES), whole),
                pl.BlockSpec((3, ROWS, NODES), whole),
                pl.BlockSpec((SLOT_ROWS, 128), lambda i, *_: (0, 0)),
            ],
            out_specs=[
                pl.BlockSpec((PAIR_BLOCK, 3, NODES), lambda i, *_: (i, 0, 0)),
                pl.BlockSpec((SLOT_ROWS, 128), lambda i, *_: (0, 0)),
                pl.BlockSpec((3, ROWS, NODES), whole),
            ],
            scratch_shapes=[
                pltpu.VMEM((4, PAIR_BLOCK, MODES, points), f32),
                pltpu.VMEM((PAIR_BLOCK, NODES, points), bf16),
                pltpu.VMEM((PAIR_BLOCK, NODES, points), bf16),
            ],
        ),
        out_shape=[
            jax.ShapeDtypeStruct((PAIRS, 3, NODES), f32),
            jax.ShapeDtypeStruct((SLOT_ROWS, 128), f32),
            jax.ShapeDtypeStruct((3, ROWS, NODES), f32),
        ],
        compiler_params=params(),
        name="mortar",
    )(slot, slave_row, coords, weights, field, load, arrived)


def as_column(line):
    tall = jnp.transpose(jnp.broadcast_to(line, (128, ROWS)))
    return jnp.concatenate([tall, tall], axis=1)


def swept(u, right, stiffness, above, below, left, right_side):
    row = lax.broadcasted_iota(jnp.int32, (ROWS, NODES), 0)
    col = lax.broadcasted_iota(jnp.int32, (ROWS, NODES), 1)
    up = jnp.where(row == 0, above, pltpu.roll(u, 1, 0))
    down = jnp.where(row == ROWS - 1, below, pltpu.roll(u, ROWS - 1, 0))
    west = jnp.where(col == 0, as_column(left), pltpu.roll(u, 1, 1))
    east = jnp.where(col == NODES - 1, as_column(right_side), pltpu.roll(u, NODES - 1, 1))
    diagonal = 4.0 + stiffness
    residual = right - (diagonal * u - (down + up + east + west))
    return u + RELAX * residual / diagonal


def put_edges(c, u, edges):
    top, bottom, left, right = edges
    top[c : c + 1, :] = u[0:1]
    bottom[c : c + 1, :] = u[ROWS - 1 : ROWS]
    left[c : c + 1, :] = jnp.transpose(u[:, 0:128])[0:1]
    right[c : c + 1, :] = jnp.transpose(u[:, 128:256])[127:128]


def slave_sweep_kernel(u_ref, right_ref, stiff_ref, ha, hb, hl, hr, out_ref, *edges):
    for c in range(3):
        u = swept(
            u_ref[c], right_ref[c], stiff_ref[...],
            ha[c : c + 1, :], hb[c : c + 1, :], hl[c : c + 1, :], hr[c : c + 1, :],
        )
        out_ref[c] = u
        put_edges(c, u, edges)


EDGES = [jax.ShapeDtypeStruct((3, 256), f32)] * 4
FIELD = jax.ShapeDtypeStruct((3, ROWS, NODES), f32)


def slave_sweep(displacement, right, stiffness, halos):
    return pl.pallas_call(
        slave_sweep_kernel,
        grid=(1,),
        out_shape=[FIELD] + EDGES,
        in_specs=[pl.BlockSpec((3, ROWS, NODES), lambda i: (0, 0, 0))] + [vmem()] * 6,
        out_specs=[vmem()] * 5,
        compiler_params=params(),
        name="slave_sweep",
    )(displacement, right, stiffness, *halos)


def master_sweep_kernel(
    asked_ref, incoming_ref, u_ref, load_ref, stiff_ref, ha, hb, hl, hr, out_ref, right_ref, *edges
):
    asked = jnp.transpose(asked_ref[...].reshape(DEVICES, 128))
    row = lax.broadcasted_iota(jnp.int32, (ROWS, DEVICES), 0)
    hits = jnp.concatenate(
        [jnp.where(row == asked[k : k + 1], 1.0, 0.0) for k in range(CAP)], axis=1
    ).astype(bf16)

    def force(part):
        lines = jnp.concatenate(
            [
                incoming_ref[pl.ds(k * PARTS + part, DEVICES, stride=CAP * PARTS), :]
                for k in range(CAP)
            ],
            axis=0,
        )
        high = lines.astype(bf16)
        low = (lines - high.astype(f32)).astype(bf16)
        dims = (((1,), (0,)), ((), ()))
        return lax.dot_general(hits, high, dims, preferred_element_type=f32) + lax.dot_general(
            hits, low, dims, preferred_element_type=f32
        )

    for c in range(3):
        right = load_ref[c] + jnp.concatenate([force(c), force(3 + c)], axis=1)
        right_ref[c] = right
        d = 3 + c
        u = swept(
            u_ref[c], right, stiff_ref[...],
            ha[d : d + 1, :], hb[d : d + 1, :], hl[d : d + 1, :], hr[d : d + 1, :],
        )
        out_ref[c] = u
        put_edges(c, u, edges)


def master_sweep(asked, incoming, displacement, load, stiffness, halos):
    second = pl.BlockSpec((3, ROWS, NODES), lambda i: (1, 0, 0))
    return pl.pallas_call(
        master_sweep_kernel,
        grid=(1,),
        out_shape=[FIELD, FIELD] + EDGES,
        in_specs=[vmem(), vmem(), second, second] + [vmem()] * 5,
        out_specs=[vmem()] * 6,
        compiler_params=params(),
        name="master_sweep",
    )(asked, incoming, displacement, load, stiffness, *halos)


def last_sweep_kernel(u_ref, right_ref, stiff_ref, ha, hb, hl, hr, *rest):
    out_ref = rest[-1]
    for c in range(3):
        out_ref[c] = swept(
            u_ref[c], right_ref[c], stiff_ref[...],
            ha[c : c + 1, :], hb[c : c + 1, :], hl[c : c + 1, :], hr[c : c + 1, :],
        )


def last_sweep(half, u, right, stiffness, halos, earlier):
    more = [] if earlier is None else [earlier]
    return pl.pallas_call(
        last_sweep_kernel,
        grid=(1,),
        out_shape=jax.ShapeDtypeStruct((6, ROWS, NODES), f32),
        in_specs=[vmem()] * 7 + [pl.BlockSpec(memory_space=pl.ANY)] * len(more),
        out_specs=pl.BlockSpec((3, ROWS, NODES), lambda i: (half, 0, 0)),
        input_output_aliases={7: 0} if more else {},
        compiler_params=params(),
        name="last_sweep",
    )(u, right, stiffness, *halos, *more)


def exchange(top, bottom, left, right):
    slabs, faces = lax.axis_size("slab"), lax.axis_size("face")
    onward = lambda n: [(i, i + 1) for i in range(n - 1)]
    back = lambda n: [(i + 1, i) for i in range(n - 1)]
    return (
        lax.ppermute(bottom, "slab", onward(slabs)),
        lax.ppermute(top, "slab", back(slabs)),
        lax.ppermute(right, "face", onward(faces)),
        lax.ppermute(left, "face", back(faces)),
    )


def all_to_all(x):
    return lax.all_to_all(x, AXES, split_axis=0, concat_axis=0, tiled=True)


def body(
    displacement,
    load,
    stiffness,
    slave_row,
    master_dev,
    master_row,
    seg_count,
    quad_coords,
    quad_weights,
):
    request, slot = slots(master_dev.reshape(1, PAIRS), master_row.reshape(1, PAIRS))
    slot = slot.reshape(PAIRS)
    asked = all_to_all(request)
    first_halos = exchange(
        displacement[:, 0, :],
        displacement[:, ROWS - 1, :],
        displacement[:, :, 0],
        displacement[:, :, NODES - 1],
    )
    active = jnp.arange(quad_weights.shape[1])[None, :] < (seg_count * QPTS)[:, None]
    weights = jnp.where(active, quad_weights, 0.0)
    coords = quad_coords.transpose(1, 0, 2)
    served = serve(asked.reshape(DEVICES * 128), displacement)
    arrived = all_to_all(served).reshape(SLOT_ROWS, 128)
    gap, outgoing, slave_right = mortar(
        slot, slave_row, coords, weights, displacement, load, arrived
    )
    incoming = all_to_all(outgoing.reshape(DEVICES, CAP * PARTS, 128)).reshape(SLOT_ROWS, 128)
    slave_u, *slave_edges = slave_sweep(displacement, slave_right, stiffness, first_halos)
    slave_done = last_sweep(0, slave_u, slave_right, stiffness, exchange(*slave_edges), None)
    master_u, master_right, *master_edges = master_sweep(
        asked, incoming, displacement, load, stiffness, first_halos
    )
    relaxed = last_sweep(
        1, master_u, master_right, stiffness, exchange(*master_edges), slave_done
    )
    return relaxed, gap


def solution(mesh):
    pairs = P(AXES)
    field = P(None, "slab", "face")
    return jax.shard_map(
        body,
        mesh=mesh,
        in_specs=(
            field,
            field,
            P("slab", "face"),
            pairs,
            P(AXES, None),
            pairs,
            pairs,
            P(AXES, None, None),
            P(AXES, None),
        ),
        out_specs=(field, P(AXES, None, None)),
        check_vma=False,
    )
```

```python
import functools

import jax
import jax.numpy as jnp
from jax import lax
from jax.experimental import pallas as pl
from jax.experimental.pallas import tpu as pltpu
from jax.sharding import PartitionSpec as P

MODES = 16
QPTS = 16
CAP = 4
PENALTY = 0.5
RELAX = 0.8
DEVICES = 128
PAIRS = 128
NODES = 256
ROWS = 256
PARTS = 6
SLOT_ROWS = DEVICES * CAP * PARTS
PAIR_BLOCK = 8

f32 = jnp.float32
bf16 = jnp.bfloat16
AXES = ("slab", "face")


def vmem():
    return pl.BlockSpec(memory_space=pltpu.VMEM)


def smem():
    return pl.BlockSpec(memory_space=pltpu.SMEM)


def params():
    return pltpu.CompilerParams(vmem_limit_bytes=48 << 20)


def slots_kernel(dev_ref, row_ref, request_ref, slot_ref):
    dev = dev_ref[...]
    row = row_ref[...]
    spread = jnp.broadcast_to(dev, (PAIRS, PAIRS))
    across = jnp.transpose(spread)
    first = lax.broadcasted_iota(jnp.int32, (PAIRS, PAIRS), 0)
    second = lax.broadcasted_iota(jnp.int32, (PAIRS, PAIRS), 1)
    same = jnp.where((spread == across) & (first < second), 1.0, 0.0)
    rank = jnp.sum(same, axis=0, keepdims=True).astype(jnp.int32)
    slot_ref[...] = dev * CAP + rank
    hits = spread == first
    result = jnp.zeros((DEVICES, 128), jnp.int32)
    for k in range(CAP):
        chosen = jnp.where(hits & (rank == k), row.astype(f32), 0.0)
        found = jnp.sum(chosen, axis=1, keepdims=True).astype(jnp.int32)
        result = jnp.where(second == k, found, result)
    request_ref[...] = result.reshape(DEVICES, 1, 128)


def slots(dev, row):
    return pl.pallas_call(
        slots_kernel,
        out_shape=[
            jax.ShapeDtypeStruct((DEVICES, 1, 128), jnp.int32),
            jax.ShapeDtypeStruct((1, PAIRS), jnp.int32),
        ],
        in_specs=[vmem(), vmem()],
        out_specs=[vmem(), vmem()],
        name="slots",
    )(dev, row)


def serve_kernel(asked_ref, field_ref, out_ref):
    def one(s, carry):
        for k in range(CAP):
            r = asked_ref[s * 128 + k]
            for c in range(3):
                line = field_ref[c, pl.ds(r, 1), :]
                out_ref[s, pl.ds(k * PARTS + c, 1), :] = line[:, 0:128]
                out_ref[s, pl.ds(k * PARTS + 3 + c, 1), :] = line[:, 128:256]
        return carry

    lax.fori_loop(0, DEVICES, one, 0, unroll=8)


def serve(asked, field):
    return pl.pallas_call(
        serve_kernel,
        grid=(1,),
        out_shape=pltpu.HBM((DEVICES, CAP * PARTS, 128), f32),
        in_specs=[smem(), pl.BlockSpec((3, ROWS, NODES), lambda i: (1, 0, 0))],
        out_specs=pl.BlockSpec((DEVICES, CAP * PARTS, 128), lambda i: (0, 0, 0)),
        compiler_params=params(),
        name="serve",
    )(asked, field)


def tables_kernel(seg_ref, coords_ref, weights_ref, out_ref, modes, slave_tab, master_tab):
    step = pl.program_id(0)
    points = weights_ref.shape[1]
    row = lax.broadcasted_iota(jnp.int32, (PAIR_BLOCK, points), 0)
    point = lax.broadcasted_iota(jnp.int32, (PAIR_BLOCK, points), 1)
    used = jnp.zeros((PAIR_BLOCK, points), jnp.int32)
    for p in range(PAIR_BLOCK):
        used = jnp.where(row == p, seg_ref[step * PAIR_BLOCK + p] * QPTS, used)
    weights = jnp.where(point < used, weights_ref[...], 0.0)
    for k in range(4):
        x = coords_ref[:, k, :]
        now = weights if k == 0 else jnp.ones_like(x)
        later = now * x
        twice = x + x
        for n in range(MODES):
            modes[k, :, n, :] = now
            now, later = later, twice * later - now

    def build(p):
        for table, along, across in ((master_tab, 2, 3), (slave_tab, 0, 1)):
            inner = modes[across, p]
            for a in range(MODES):
                outer = modes[along, p, a : a + 1, :]
                table[p, a * MODES : (a + 1) * MODES, :] = (inner * outer).astype(bf16)

    def emit(p):
        turned = lax.dot_general(
            master_tab[p], slave_tab[p], (((1,), (1,)), ((), ())), preferred_element_type=f32
        )
        high = turned.astype(bf16)
        out_ref[p, :, 0:NODES] = high
        out_ref[p, :, NODES : 2 * NODES] = (turned - high.astype(f32)).astype(bf16)

    build(0)
    for p in range(PAIR_BLOCK):
        if p + 1 < PAIR_BLOCK:
            build(p + 1)
        emit(p)


def couple_tables(seg_count, coords, weights):
    points = weights.shape[1]
    return pl.pallas_call(
        tables_kernel,
        grid_spec=pltpu.PrefetchScalarGridSpec(
            num_scalar_prefetch=1,
            grid=(PAIRS // PAIR_BLOCK,),
            in_specs=[
                pl.BlockSpec((PAIR_BLOCK, 4, points), lambda i, *_: (i, 0, 0)),
                pl.BlockSpec((PAIR_BLOCK, points), lambda i, *_: (i, 0)),
            ],
            out_specs=pl.BlockSpec((PAIR_BLOCK, NODES, 2 * NODES), lambda i, *_: (i, 0, 0)),
            scratch_shapes=[
                pltpu.VMEM((4, PAIR_BLOCK, MODES, points), f32),
                pltpu.VMEM((PAIR_BLOCK, NODES, points), bf16),
                pltpu.VMEM((PAIR_BLOCK, NODES, points), bf16),
            ],
        ),
        out_shape=jax.ShapeDtypeStruct((PAIRS, NODES, 2 * NODES), bf16),
        compiler_params=pltpu.CompilerParams(vmem_limit_bytes=32 << 20),
        cost_estimate=pl.CostEstimate(
            flops=2 * PAIRS * NODES * NODES * points, bytes_accessed=64 << 20, transcendentals=0
        ),
        name="couple_tables",
    )(seg_count, coords, weights)


def two_pieces(u):
    high = u.astype(bf16)
    low = u - high.astype(f32)
    return jnp.concatenate([high.astype(f32), low], axis=0).astype(bf16)


def times(pieces, table):
    both = lax.dot_general(pieces, table, (((1,), (0,)), ((), ())), preferred_element_type=f32)
    return both[0:8] + both[8:16]


COUPLE_BLOCK = 16
LAG = 2


def couple_kernel(
    slot_ref, row_ref, turned_ref, field_ref, load_ref, arrived_ref, gap_ref, outgoing_ref, right_ref
):
    step = pl.program_id(0)

    @pl.when(step == 0)
    def _():
        outgoing_ref[...] = jnp.zeros_like(outgoing_ref)
        right_ref[...] = load_ref[...]

    rest = jnp.zeros((5, NODES), f32)
    held = {}

    def pull(p):
        pair = step * COUPLE_BLOCK + p
        both = arrived_ref[pl.ds(slot_ref[pair] * PARTS, PARTS), :]
        u = jnp.concatenate([both[0:3], both[3:6]], axis=1)
        u = two_pieces(jnp.concatenate([u, rest], axis=0))
        pulled = times(u, turned_ref[p, :, 0:NODES])
        pulled = pulled + times(u, turned_ref[p, :, NODES : 2 * NODES])
        r = row_ref[pair]
        lines = [field_ref[c, pl.ds(r, 1), :] for c in range(3)]
        gap = jnp.concatenate(lines + [rest], axis=0) - pulled
        half = PENALTY * gap
        for c in range(3):
            gap_ref[c, p : p + 1, :] = gap[c : c + 1]
            right_ref[c, pl.ds(r, 1), :] = right_ref[c, pl.ds(r, 1), :] - half[c : c + 1]
        pieces = two_pieces(half)
        held[p] = jnp.concatenate([pieces, pieces], axis=1)

    def push(p):
        pair = step * COUPLE_BLOCK + p
        both = lax.dot_general(
            turned_ref[p], held[p], (((1,), (1,)), ((), ())), preferred_element_type=f32
        )
        both = jnp.transpose(both)
        back = both[0:8] + both[8:16]
        outgoing_ref[pl.ds(slot_ref[pair] * PARTS, PARTS), :] = jnp.concatenate(
            [back[0:3, 0:128], back[0:3, 128:256]], axis=0
        )

    for p in range(COUPLE_BLOCK + LAG):
        if p < COUPLE_BLOCK:
            pull(p)
        if p >= LAG:
            push(p - LAG)


def couple(slot, slave_row, turned, field, load, arrived):
    whole = lambda i, *_: (0, 0, 0)
    return pl.pallas_call(
        couple_kernel,
        grid_spec=pltpu.PrefetchScalarGridSpec(
            num_scalar_prefetch=2,
            grid=(PAIRS // COUPLE_BLOCK,),
            in_specs=[
                pl.BlockSpec((COUPLE_BLOCK, NODES, 2 * NODES), lambda i, *_: (i, 0, 0)),
                pl.BlockSpec((3, ROWS, NODES), whole),
                pl.BlockSpec((3, ROWS, NODES), whole),
                pl.BlockSpec((SLOT_ROWS, 128), lambda i, *_: (0, 0)),
            ],
            out_specs=[
                pl.BlockSpec((3, COUPLE_BLOCK, NODES), lambda i, *_: (0, i, 0)),
                pl.BlockSpec((SLOT_ROWS, 128), lambda i, *_: (0, 0)),
                pl.BlockSpec((3, ROWS, NODES), whole),
            ],
        ),
        out_shape=[
            pltpu.HBM((3, PAIRS, NODES), f32),
            pltpu.HBM((SLOT_ROWS, 128), f32),
            jax.ShapeDtypeStruct((3, ROWS, NODES), f32),
        ],
        compiler_params=pltpu.CompilerParams(vmem_limit_bytes=40 << 20),
        name="couple",
    )(slot, slave_row, turned, field, load, arrived)


def as_column(line):
    tall = jnp.transpose(jnp.broadcast_to(line, (128, ROWS)))
    return jnp.concatenate([tall, tall], axis=1)


def swept(u, right, stiffness, above, below, left, right_side):
    row = lax.broadcasted_iota(jnp.int32, (ROWS, NODES), 0)
    col = lax.broadcasted_iota(jnp.int32, (ROWS, NODES), 1)
    up = jnp.where(row == 0, above, pltpu.roll(u, 1, 0))
    down = jnp.where(row == ROWS - 1, below, pltpu.roll(u, ROWS - 1, 0))
    west = jnp.where(col == 0, as_column(left), pltpu.roll(u, 1, 1))
    east = jnp.where(col == NODES - 1, as_column(right_side), pltpu.roll(u, NODES - 1, 1))
    diagonal = 4.0 + stiffness
    residual = right - (diagonal * u - (down + up + east + west))
    return u + RELAX * residual / diagonal


def put_edges(c, u, edges):
    top, bottom, left, right = edges
    top[c : c + 1, :] = u[0:1]
    bottom[c : c + 1, :] = u[ROWS - 1 : ROWS]
    left[c : c + 1, :] = jnp.transpose(u[:, 0:128])[0:1]
    right[c : c + 1, :] = jnp.transpose(u[:, 128:256])[127:128]


def slave_sweep_kernel(u_ref, right_ref, stiff_ref, ha, hb, hl, hr, out_ref, *edges):
    for c in range(3):
        u = swept(
            u_ref[c], right_ref[c], stiff_ref[...],
            ha[c : c + 1, :], hb[c : c + 1, :], hl[c : c + 1, :], hr[c : c + 1, :],
        )
        out_ref[c] = u
        put_edges(c, u, edges)


def edges_kernel(u_ref, *edges):
    for c in range(6):
        put_edges(c, u_ref[c], edges)


def first_edges(displacement):
    return pl.pallas_call(
        edges_kernel,
        out_shape=[jax.ShapeDtypeStruct((6, 256), f32)] * 4,
        in_specs=[vmem()],
        out_specs=[vmem()] * 4,
        compiler_params=params(),
        name="first_edges",
    )(displacement)


EDGES = [jax.ShapeDtypeStruct((3, 256), f32)] * 4
FIELD = jax.ShapeDtypeStruct((3, ROWS, NODES), f32)


def slave_sweep(displacement, right, stiffness, halos):
    return pl.pallas_call(
        slave_sweep_kernel,
        grid=(1,),
        out_shape=[FIELD] + EDGES,
        in_specs=[pl.BlockSpec((3, ROWS, NODES), lambda i: (0, 0, 0))] + [vmem()] * 6,
        out_specs=[vmem()] * 5,
        compiler_params=params(),
        name="slave_sweep",
    )(displacement, right, stiffness, *halos)


def master_sweep_kernel(
    asked_ref, incoming_ref, u_ref, load_ref, stiff_ref, ha, hb, hl, hr, ea, eb, el, er,
    out_ref, right_ref, *edges
):
    asked = jnp.transpose(asked_ref[...].reshape(DEVICES, 128))
    row = lax.broadcasted_iota(jnp.int32, (ROWS, DEVICES), 0)
    hits = jnp.concatenate(
        [jnp.where(row == asked[k : k + 1], 1.0, 0.0) for k in range(CAP)], axis=1
    ).astype(bf16)

    def force(part):
        lines = jnp.concatenate(
            [
                incoming_ref[pl.ds(k * PARTS + part, DEVICES, stride=CAP * PARTS), :]
                for k in range(CAP)
            ],
            axis=0,
        )
        high = lines.astype(bf16)
        low = (lines - high.astype(f32)).astype(bf16)
        dims = (((1,), (0,)), ((), ()))
        return lax.dot_general(hits, high, dims, preferred_element_type=f32) + lax.dot_general(
            hits, low, dims, preferred_element_type=f32
        )

    for edge, slave_edge in zip(edges, (ea, eb, el, er)):
        edge[0:3, :] = slave_edge[...]
    for c in range(3):
        right = load_ref[c] + jnp.concatenate([force(c), force(3 + c)], axis=1)
        right_ref[c] = right
        d = 3 + c
        u = swept(
            u_ref[c], right, stiff_ref[...],
            ha[d : d + 1, :], hb[d : d + 1, :], hl[d : d + 1, :], hr[d : d + 1, :],
        )
        out_ref[c] = u
        put_edges(d, u, edges)


def master_sweep(asked, incoming, displacement, load, stiffness, halos, slave_edges):
    second = pl.BlockSpec((3, ROWS, NODES), lambda i: (1, 0, 0))
    return pl.pallas_call(
        master_sweep_kernel,
        grid=(1,),
        out_shape=[FIELD, FIELD] + [jax.ShapeDtypeStruct((6, 256), f32)] * 4,
        in_specs=[vmem(), vmem(), second, second] + [vmem()] * 9,
        out_specs=[vmem()] * 6,
        compiler_params=params(),
        name="master_sweep",
    )(asked, incoming, displacement, load, stiffness, *halos, *slave_edges)


def last_sweep_kernel(us_ref, rs_ref, um_ref, rm_ref, stiff_ref, ha, hb, hl, hr, out_ref):
    for c in range(6):
        u_ref, right_ref = (us_ref, rs_ref) if c < 3 else (um_ref, rm_ref)
        out_ref[c] = swept(
            u_ref[c % 3], right_ref[c % 3], stiff_ref[...],
            ha[c : c + 1, :], hb[c : c + 1, :], hl[c : c + 1, :], hr[c : c + 1, :],
        )


def last_sweep(slave_u, slave_right, master_u, master_right, stiffness, halos):
    return pl.pallas_call(
        last_sweep_kernel,
        out_shape=jax.ShapeDtypeStruct((6, ROWS, NODES), f32),
        in_specs=[vmem()] * 9,
        out_specs=vmem(),
        compiler_params=params(),
        name="last_sweep",
    )(slave_u, slave_right, master_u, master_right, stiffness, *halos)


def exchange(top, bottom, left, right):
    slabs, faces = lax.axis_size("slab"), lax.axis_size("face")
    onward = lambda n: [(i, i + 1) for i in range(n - 1)]
    back = lambda n: [(i + 1, i) for i in range(n - 1)]
    return (
        lax.ppermute(bottom, "slab", onward(slabs)),
        lax.ppermute(top, "slab", back(slabs)),
        lax.ppermute(right, "face", onward(faces)),
        lax.ppermute(left, "face", back(faces)),
    )


def all_to_all(x):
    return lax.all_to_all(x, AXES, split_axis=0, concat_axis=0, tiled=True)


def body(
    displacement,
    load,
    stiffness,
    slave_row,
    master_dev,
    master_row,
    seg_count,
    quad_coords,
    quad_weights,
):
    request, slot = slots(master_dev.reshape(1, PAIRS), master_row.reshape(1, PAIRS))
    slot = slot.reshape(PAIRS)
    asked = all_to_all(request)
    first_halos = exchange(*first_edges(displacement))
    turned = couple_tables(seg_count, quad_coords, quad_weights)
    served = serve(asked.reshape(DEVICES * 128), displacement)
    arrived = all_to_all(served).reshape(SLOT_ROWS, 128)
    gap, outgoing, slave_right = couple(slot, slave_row, turned, displacement, load, arrived)
    incoming = all_to_all(outgoing.reshape(DEVICES, CAP * PARTS, 128)).reshape(SLOT_ROWS, 128)
    slave_u, *slave_edges = slave_sweep(displacement, slave_right, stiffness, first_halos)
    master_u, master_right, *edges = master_sweep(
        asked, incoming, displacement, load, stiffness, first_halos, slave_edges
    )
    relaxed = last_sweep(
        slave_u, slave_right, master_u, master_right, stiffness, exchange(*edges)
    )
    return relaxed, gap.transpose(1, 0, 2)


def solution(mesh):
    pairs = P(AXES)
    field = P(None, "slab", "face")
    return jax.shard_map(
        body,
        mesh=mesh,
        in_specs=(
            field,
            field,
            P("slab", "face"),
            pairs,
            P(AXES, None),
            pairs,
            pairs,
            P(AXES, None, None),
            P(AXES, None),
        ),
        out_specs=(field, P(AXES, None, None)),
        check_vma=False,
    )
```

```python
import functools

import jax
import jax.numpy as jnp
from jax import lax
from jax.experimental import pallas as pl
from jax.experimental.pallas import tpu as pltpu
from jax.sharding import PartitionSpec as P

MODES = 16
QPTS = 16
CAP = 4
PENALTY = 0.5
RELAX = 0.8
DEVICES = 128
PAIRS = 128
NODES = 256
ROWS = 256
PARTS = 6
SLOT_ROWS = DEVICES * CAP * PARTS
PAIR_BLOCK = 8

f32 = jnp.float32
bf16 = jnp.bfloat16
f8 = jnp.float8_e5m2
REST_SCALE = 4096.0
AXES = ("slab", "face")


def vmem():
    return pl.BlockSpec(memory_space=pltpu.VMEM)


def smem():
    return pl.BlockSpec(memory_space=pltpu.SMEM)


def in_hbm(x):
    return pltpu.with_memory_space_constraint(x, pltpu.HBM)


def params():
    return pltpu.CompilerParams(vmem_limit_bytes=48 << 20)


def slots_kernel(dev_ref, row_ref, request_ref, slot_ref):
    dev = dev_ref[...]
    row = row_ref[...]
    spread = jnp.broadcast_to(dev, (PAIRS, PAIRS))
    across = jnp.transpose(spread)
    first = lax.broadcasted_iota(jnp.int32, (PAIRS, PAIRS), 0)
    second = lax.broadcasted_iota(jnp.int32, (PAIRS, PAIRS), 1)
    same = jnp.where((spread == across) & (first < second), 1.0, 0.0)
    rank = jnp.sum(same, axis=0, keepdims=True).astype(jnp.int32)
    slot_ref[...] = dev * CAP + rank
    hits = spread == first
    result = jnp.zeros((DEVICES, 128), jnp.int32)
    for k in range(CAP):
        chosen = jnp.where(hits & (rank == k), row.astype(f32), 0.0)
        found = jnp.sum(chosen, axis=1, keepdims=True).astype(jnp.int32)
        result = jnp.where(second == k, found, result)
    request_ref[...] = result.reshape(DEVICES, 1, 128)


def slots(dev, row):
    return pl.pallas_call(
        slots_kernel,
        out_shape=[
            jax.ShapeDtypeStruct((DEVICES, 1, 128), jnp.int32),
            jax.ShapeDtypeStruct((1, PAIRS), jnp.int32),
        ],
        in_specs=[vmem(), vmem()],
        out_specs=[vmem(), vmem()],
        name="slots",
    )(dev, row)


def serve_kernel(asked_ref, field_ref, out_ref):
    def one(s, carry):
        for k in range(CAP):
            r = asked_ref[s * 128 + k]
            for c in range(3):
                line = field_ref[c, pl.ds(r, 1), :]
                out_ref[s, pl.ds(k * PARTS + c, 1), :] = line[:, 0:128]
                out_ref[s, pl.ds(k * PARTS + 3 + c, 1), :] = line[:, 128:256]
        return carry

    lax.fori_loop(0, DEVICES, one, 0, unroll=8)


def serve(asked, field):
    return pl.pallas_call(
        serve_kernel,
        grid=(1,),
        out_shape=pltpu.HBM((DEVICES, CAP * PARTS, 128), f32),
        in_specs=[
            smem(),
            pl.BlockSpec((3, ROWS, NODES), lambda i: (1, 0, 0)),
        ],
        out_specs=pl.BlockSpec((DEVICES, CAP * PARTS, 128), lambda i: (0, 0, 0)),
        compiler_params=params(),
        name="serve",
    )(asked, in_hbm(field))


def tables_kernel(
    seg_ref, coords_ref, weights_ref, high_ref, rest_ref, modes, slave_tab, master_tab
):
    step = pl.program_id(0)
    points = weights_ref.shape[1]
    row = lax.broadcasted_iota(jnp.int32, (PAIR_BLOCK, points), 0)
    point = lax.broadcasted_iota(jnp.int32, (PAIR_BLOCK, points), 1)
    used = jnp.zeros((PAIR_BLOCK, points), jnp.int32)
    for p in range(PAIR_BLOCK):
        used = jnp.where(row == p, seg_ref[step * PAIR_BLOCK + p] * QPTS, used)
    weights = jnp.where(point < used, weights_ref[...], 0.0)
    for k in range(4):
        x = coords_ref[:, k, :]
        now = weights if k == 0 else jnp.ones_like(x)
        later = now * x
        twice = x + x
        for n in range(MODES):
            modes[k, :, n, :] = now
            now, later = later, twice * later - now

    def build(p):
        for table, along, across in ((master_tab, 2, 3), (slave_tab, 0, 1)):
            inner = modes[across, p]
            for a in range(MODES):
                outer = modes[along, p, a : a + 1, :]
                table[p, a * MODES : (a + 1) * MODES, :] = (inner * outer).astype(bf16)

    def emit(p):
        turned = lax.dot_general(
            master_tab[p], slave_tab[p], (((1,), (1,)), ((), ())), preferred_element_type=f32
        )
        high = turned.astype(bf16)
        high_ref[p] = high
        rest_ref[p] = ((turned - high.astype(f32)) * REST_SCALE).astype(f8)

    build(0)
    for p in range(PAIR_BLOCK):
        if p + 1 < PAIR_BLOCK:
            build(p + 1)
        emit(p)


def couple_tables(seg_count, coords, weights):
    points = weights.shape[1]
    block = pl.BlockSpec((PAIR_BLOCK, NODES, NODES), lambda i, *_: (i, 0, 0))
    return pl.pallas_call(
        tables_kernel,
        grid_spec=pltpu.PrefetchScalarGridSpec(
            num_scalar_prefetch=1,
            grid=(PAIRS // PAIR_BLOCK,),
            in_specs=[
                pl.BlockSpec((PAIR_BLOCK, 4, points), lambda i, *_: (i, 0, 0)),
                pl.BlockSpec((PAIR_BLOCK, points), lambda i, *_: (i, 0)),
            ],
            out_specs=[block, block],
            scratch_shapes=[
                pltpu.VMEM((4, PAIR_BLOCK, MODES, points), f32),
                pltpu.VMEM((PAIR_BLOCK, NODES, points), bf16),
                pltpu.VMEM((PAIR_BLOCK, NODES, points), bf16),
            ],
        ),
        out_shape=[
            pltpu.HBM((PAIRS, NODES, NODES), bf16),
            pltpu.HBM((PAIRS, NODES, NODES), f8),
        ],
        compiler_params=pltpu.CompilerParams(vmem_limit_bytes=32 << 20),
        cost_estimate=pl.CostEstimate(
            flops=8 * PAIRS * NODES * NODES * points, bytes_accessed=64 << 20, transcendentals=0
        ),
        name="couple_tables",
    )(seg_count, in_hbm(coords), in_hbm(weights))


def two_pieces(u):
    high = u.astype(bf16)
    low = u - high.astype(f32)
    return jnp.concatenate([high.astype(f32), low], axis=0).astype(bf16)


def two_small_pieces(u):
    high = u.astype(f8).astype(f32)
    return jnp.concatenate([high, u - high, jnp.zeros((16, u.shape[1]), f32)], axis=0).astype(f8)


def times(pieces, table):
    both = lax.dot_general(pieces, table, (((1,), (0,)), ((), ())), preferred_element_type=f32)
    return both[0:8] + both[8:16]


def times_turned(pieces, table):
    both = lax.dot_general(table, pieces, (((1,), (1,)), ((), ())), preferred_element_type=f32)
    both = jnp.transpose(both)
    return both[0:8] + both[8:16]


COUPLE_BLOCK = 16
SLOTS = 4


def couple_kernel(
    slot_ref, row_ref, high_ref, rest_ref, field_ref, arrived_ref,
    gap_ref, back_ref, highs, rests, held, held_small, sems,
):
    count = PAIRS // COUPLE_BLOCK

    def copies(block):
        room = lax.rem(block, SLOTS)
        here = pl.ds(block * COUPLE_BLOCK, COUPLE_BLOCK)
        return (
            pltpu.make_async_copy(high_ref.at[here], highs.at[room], sems.at[0, room]),
            pltpu.make_async_copy(rest_ref.at[here], rests.at[room], sems.at[1, room]),
        )

    def start(block):
        for copy in copies(block):
            copy.start()

    def wait(block):
        for copy in copies(block):
            copy.wait()

    empty = jnp.zeros((5, NODES), f32)

    def pull(block, p):
        room = lax.rem(block, SLOTS)
        pair = block * COUPLE_BLOCK + p
        both = arrived_ref[pl.ds(slot_ref[pair] * PARTS, PARTS), :]
        u = jnp.concatenate([both[0:3], both[3:6]], axis=1)
        u = jnp.concatenate([u, empty], axis=0)
        pulled = times(two_pieces(u), highs[room, p])
        pulled = pulled + times(two_small_pieces(u), rests[room, p]) * (1.0 / REST_SCALE)
        r = row_ref[pair]
        lines = [field_ref[c, pl.ds(r, 1), :] for c in range(3)]
        gap = jnp.concatenate(lines + [empty], axis=0) - pulled
        for c in range(3):
            gap_ref[c, pl.ds(pair, 1), :] = gap[c : c + 1]
        half = PENALTY * gap
        held[p] = two_pieces(half)
        held_small[p] = two_small_pieces(half)

    def push(block, p):
        room = lax.rem(block, SLOTS)
        back = times_turned(held[p], highs[room, p])
        back = back + times_turned(held_small[p], rests[room, p]) * (1.0 / REST_SCALE)
        back_ref[pl.ds(slot_ref[block * COUPLE_BLOCK + p] * PARTS, PARTS), :] = jnp.concatenate(
            [back[0:3, 0:128], back[0:3, 128:256]], axis=0
        )

    for ahead in range(SLOTS - 1):
        start(ahead)
    back_ref[...] = jnp.zeros_like(back_ref)
    wait(0)
    for p in range(COUPLE_BLOCK):
        pull(0, p)

    def one(block, carry):
        wait(block)

        @pl.when(block + SLOTS - 2 < count)
        def _():
            start(block + SLOTS - 2)

        for p in range(COUPLE_BLOCK):
            push(block - 1, p)
            pull(block, p)
        return carry

    lax.fori_loop(1, count, one, 0)
    for p in range(COUPLE_BLOCK):
        push(count - 1, p)


def couple(slot, slave_row, turned, field, arrived):
    whole = lambda *_: (0, 0, 0)
    flat = pl.BlockSpec((SLOT_ROWS, 128), lambda *_: (0, 0))
    anywhere = pl.BlockSpec(memory_space=pl.ANY)
    return pl.pallas_call(
        couple_kernel,
        grid_spec=pltpu.PrefetchScalarGridSpec(
            num_scalar_prefetch=2,
            grid=(1,),
            in_specs=[anywhere, anywhere, pl.BlockSpec((3, ROWS, NODES), whole), flat],
            out_specs=[pl.BlockSpec((3, PAIRS, NODES), whole), flat],
            scratch_shapes=[
                pltpu.VMEM((SLOTS, COUPLE_BLOCK, NODES, NODES), bf16),
                pltpu.VMEM((SLOTS, COUPLE_BLOCK, NODES, NODES), f8),
                pltpu.VMEM((COUPLE_BLOCK, 16, NODES), bf16),
                pltpu.VMEM((COUPLE_BLOCK, 32, NODES), f8),
                pltpu.SemaphoreType.DMA((2, SLOTS)),
            ],
        ),
        out_shape=[
            pltpu.HBM((3, PAIRS, NODES), f32),
            pltpu.HBM((SLOT_ROWS, 128), f32),
        ],
        compiler_params=params(),
        name="couple",
    )(slot, slave_row, *turned, in_hbm(field), in_hbm(arrived))


def gathered(hits, lines):
    high = lines.astype(bf16)
    low = (lines - high.astype(f32)).astype(bf16)
    dims = (((1,), (0,)), ((), ()))
    return lax.dot_general(hits, high, dims, preferred_element_type=f32) + lax.dot_general(
        hits, low, dims, preferred_element_type=f32
    )


def as_column(line):
    tall = jnp.transpose(jnp.broadcast_to(line, (128, ROWS)))
    return jnp.concatenate([tall, tall], axis=1)


def swept(u, right, stiffness, above, below, left, right_side):
    row = lax.broadcasted_iota(jnp.int32, (ROWS, NODES), 0)
    col = lax.broadcasted_iota(jnp.int32, (ROWS, NODES), 1)
    up = jnp.where(row == 0, above, pltpu.roll(u, 1, 0))
    down = jnp.where(row == ROWS - 1, below, pltpu.roll(u, ROWS - 1, 0))
    west = jnp.where(col == 0, as_column(left), pltpu.roll(u, 1, 1))
    east = jnp.where(col == NODES - 1, as_column(right_side), pltpu.roll(u, NODES - 1, 1))
    diagonal = 4.0 + stiffness
    residual = right - (diagonal * u - (down + up + east + west))
    return u + RELAX * residual / diagonal


def put_edges(c, u, edges):
    top, bottom, left, right = edges
    top[c : c + 1, :] = u[0:1]
    bottom[c : c + 1, :] = u[ROWS - 1 : ROWS]
    left[c : c + 1, :] = jnp.transpose(u[:, 0:128])[0:1]
    right[c : c + 1, :] = jnp.transpose(u[:, 128:256])[127:128]


def slave_sweep_kernel(
    row_ref, gap_ref, u_ref, load_ref, stiff_ref, ha, hb, hl, hr, out_ref, right_ref, *edges
):
    row = lax.broadcasted_iota(jnp.int32, (ROWS, PAIRS), 0)
    hits = jnp.where(row == row_ref[...], 1.0, 0.0).astype(bf16)
    for c in range(3):
        right = load_ref[c] - PENALTY * gathered(hits, gap_ref[c])
        right_ref[c] = right
        u = swept(
            u_ref[c], right, stiff_ref[...],
            ha[c : c + 1, :], hb[c : c + 1, :], hl[c : c + 1, :], hr[c : c + 1, :],
        )
        out_ref[c] = u
        put_edges(c, u, edges)


def edges_kernel(u_ref, *edges):
    for c in range(6):
        put_edges(c, u_ref[c], edges)


def first_edges(displacement):
    return pl.pallas_call(
        edges_kernel,
        out_shape=[jax.ShapeDtypeStruct((6, 256), f32)] * 4,
        in_specs=[vmem()],
        out_specs=[vmem()] * 4,
        compiler_params=params(),
        name="first_edges",
    )(displacement)


EDGES = [jax.ShapeDtypeStruct((3, 256), f32)] * 4
FIELD = jax.ShapeDtypeStruct((3, ROWS, NODES), f32)


def slave_sweep(slave_row, gap, displacement, load, stiffness, halos):
    half = pl.BlockSpec((3, ROWS, NODES), lambda i: (0, 0, 0))
    return pl.pallas_call(
        slave_sweep_kernel,
        grid=(1,),
        out_shape=[FIELD, FIELD] + EDGES,
        in_specs=[vmem(), vmem(), half, half] + [vmem()] * 5,
        out_specs=[vmem()] * 6,
        compiler_params=params(),
        name="slave_sweep",
    )(slave_row, gap, in_hbm(displacement), in_hbm(load), stiffness, *halos)


def master_sweep_kernel(
    asked_ref, incoming_ref, u_ref, load_ref, stiff_ref, ha, hb, hl, hr, ea, eb, el, er,
    out_ref, right_ref, *edges
):
    asked = jnp.transpose(asked_ref[...].reshape(DEVICES, 128))
    row = lax.broadcasted_iota(jnp.int32, (ROWS, DEVICES), 0)
    hits = jnp.concatenate(
        [jnp.where(row == asked[k : k + 1], 1.0, 0.0) for k in range(CAP)], axis=1
    ).astype(bf16)

    def force(part):
        lines = jnp.concatenate(
            [
                incoming_ref[pl.ds(k * PARTS + part, DEVICES, stride=CAP * PARTS), :]
                for k in range(CAP)
            ],
            axis=0,
        )
        return gathered(hits, lines)

    for edge, slave_edge in zip(edges, (ea, eb, el, er)):
        edge[0:3, :] = slave_edge[...]
    for c in range(3):
        right = load_ref[c] + jnp.concatenate([force(c), force(3 + c)], axis=1)
        right_ref[c] = right
        d = 3 + c
        u = swept(
            u_ref[c], right, stiff_ref[...],
            ha[d : d + 1, :], hb[d : d + 1, :], hl[d : d + 1, :], hr[d : d + 1, :],
        )
        out_ref[c] = u
        put_edges(d, u, edges)


def master_sweep(asked, incoming, displacement, load, stiffness, halos, slave_edges):
    second = pl.BlockSpec((3, ROWS, NODES), lambda i: (1, 0, 0))
    return pl.pallas_call(
        master_sweep_kernel,
        grid=(1,),
        out_shape=[FIELD, FIELD] + [jax.ShapeDtypeStruct((6, 256), f32)] * 4,
        in_specs=[vmem(), vmem(), second, second] + [vmem()] * 9,
        out_specs=[vmem()] * 6,
        compiler_params=params(),
        name="master_sweep",
    )(asked, incoming, in_hbm(displacement), in_hbm(load), stiffness, *halos, *slave_edges)


def last_sweep_kernel(us_ref, rs_ref, um_ref, rm_ref, stiff_ref, ha, hb, hl, hr, out_ref):
    for c in range(6):
        u_ref, right_ref = (us_ref, rs_ref) if c < 3 else (um_ref, rm_ref)
        out_ref[c] = swept(
            u_ref[c % 3], right_ref[c % 3], stiff_ref[...],
            ha[c : c + 1, :], hb[c : c + 1, :], hl[c : c + 1, :], hr[c : c + 1, :],
        )


def last_sweep(slave_u, slave_right, master_u, master_right, stiffness, halos):
    return pl.pallas_call(
        last_sweep_kernel,
        out_shape=jax.ShapeDtypeStruct((6, ROWS, NODES), f32),
        in_specs=[vmem()] * 9,
        out_specs=vmem(),
        compiler_params=params(),
        name="last_sweep",
    )(slave_u, slave_right, master_u, master_right, stiffness, *halos)


def exchange(top, bottom, left, right):
    slabs, faces = lax.axis_size("slab"), lax.axis_size("face")
    onward = lambda n: [(i, i + 1) for i in range(n - 1)]
    back = lambda n: [(i + 1, i) for i in range(n - 1)]
    return (
        lax.ppermute(bottom, "slab", onward(slabs)),
        lax.ppermute(top, "slab", back(slabs)),
        lax.ppermute(right, "face", onward(faces)),
        lax.ppermute(left, "face", back(faces)),
    )


def all_to_all(x):
    return lax.all_to_all(x, AXES, split_axis=0, concat_axis=0, tiled=True)


def body(
    displacement,
    load,
    stiffness,
    slave_row,
    master_dev,
    master_row,
    seg_count,
    quad_coords,
    quad_weights,
):
    request, slot = slots(master_dev.reshape(1, PAIRS), master_row.reshape(1, PAIRS))
    slot = slot.reshape(PAIRS)
    asked = all_to_all(request)
    first_halos = exchange(*first_edges(displacement))
    turned = couple_tables(seg_count, quad_coords, quad_weights)
    served = serve(asked.reshape(DEVICES * 128), displacement)
    arrived = all_to_all(served).reshape(SLOT_ROWS, 128)
    gap, outgoing = couple(slot, slave_row, turned, displacement, arrived)
    incoming = all_to_all(outgoing.reshape(DEVICES, CAP * PARTS, 128)).reshape(SLOT_ROWS, 128)
    slave_u, slave_right, *slave_edges = slave_sweep(
        slave_row.reshape(1, PAIRS), gap, displacement, load, stiffness, first_halos
    )
    master_u, master_right, *edges = master_sweep(
        asked, incoming, displacement, load, stiffness, first_halos, slave_edges
    )
    relaxed = last_sweep(
        slave_u, slave_right, master_u, master_right, stiffness, exchange(*edges)
    )
    return relaxed, gap.transpose(1, 0, 2)


def solution(mesh):
    pairs = P(AXES)
    field = P(None, "slab", "face")
    return jax.shard_map(
        body,
        mesh=mesh,
        in_specs=(
            field,
            field,
            P("slab", "face"),
            pairs,
            P(AXES, None),
            pairs,
            pairs,
            P(AXES, None, None),
            P(AXES, None),
        ),
        out_specs=(field, P(AXES, None, None)),
        check_vma=False,
    )
```

```python
import functools

import jax
import jax.numpy as jnp
from jax import lax
from jax.experimental import pallas as pl
from jax.experimental.pallas import tpu as pltpu
from jax.sharding import PartitionSpec as P

MODES = 16
QPTS = 16
CAP = 4
PENALTY = 0.5
RELAX = 0.8
DEVICES = 128
PAIRS = 128
NODES = 256
ROWS = 256
PARTS = 6
SLOT_ROWS = DEVICES * CAP * PARTS
PAIR_BLOCK = 8

f32 = jnp.float32
bf16 = jnp.bfloat16
f8 = jnp.float8_e5m2
REST_SCALE = 4096.0
AXES = ("slab", "face")


def vmem():
    return pl.BlockSpec(memory_space=pltpu.VMEM)


def smem():
    return pl.BlockSpec(memory_space=pltpu.SMEM)


def in_vmem(x):
    return pltpu.with_memory_space_constraint(x, pltpu.VMEM)


def in_hbm(x):
    return pltpu.with_memory_space_constraint(x, pltpu.HBM)


def params():
    return pltpu.CompilerParams(vmem_limit_bytes=48 << 20)


def slots_kernel(dev_ref, row_ref, request_ref, slot_ref):
    dev = dev_ref[...]
    row = row_ref[...]
    spread = jnp.broadcast_to(dev, (PAIRS, PAIRS))
    across = jnp.transpose(spread)
    first = lax.broadcasted_iota(jnp.int32, (PAIRS, PAIRS), 0)
    second = lax.broadcasted_iota(jnp.int32, (PAIRS, PAIRS), 1)
    same = jnp.where((spread == across) & (first < second), 1.0, 0.0)
    rank = jnp.sum(same, axis=0, keepdims=True).astype(jnp.int32)
    slot_ref[...] = dev * CAP + rank
    hits = spread == first
    result = jnp.zeros((DEVICES, 128), jnp.int32)
    for k in range(CAP):
        chosen = jnp.where(hits & (rank == k), row.astype(f32), 0.0)
        found = jnp.sum(chosen, axis=1, keepdims=True).astype(jnp.int32)
        result = jnp.where(second == k, found, result)
    request_ref[...] = result.reshape(DEVICES, 1, 128)


def slots(dev, row):
    return pl.pallas_call(
        slots_kernel,
        out_shape=[
            jax.ShapeDtypeStruct((DEVICES, 1, 128), jnp.int32),
            jax.ShapeDtypeStruct((1, PAIRS), jnp.int32),
        ],
        in_specs=[vmem(), vmem()],
        out_specs=[vmem(), vmem()],
        name="slots",
    )(dev, row)


SERVE_STEPS = 2


def serve_kernel(asked_ref, field_ref, out_ref):
    begin = pl.program_id(0) * (DEVICES // SERVE_STEPS)

    def one(s, carry):
        lines = []
        for k in range(CAP):
            r = asked_ref[(begin + s) * 128 + k]
            lines.append([field_ref[c, pl.ds(r, 1), :] for c in range(3)])
        out_ref[s] = jnp.concatenate(
            [
                line[:, h * 128 : h * 128 + 128]
                for k in range(CAP)
                for h in range(2)
                for line in lines[k]
            ],
            axis=0,
        )
        return carry

    lax.fori_loop(0, DEVICES // SERVE_STEPS, one, 0, unroll=8)


def serve(asked, field):
    return pl.pallas_call(
        serve_kernel,
        grid=(SERVE_STEPS,),
        out_shape=pltpu.HBM((DEVICES, CAP * PARTS, 128), f32),
        in_specs=[smem(), pl.BlockSpec((3, ROWS, NODES), lambda i: (1, 0, 0))],
        out_specs=pl.BlockSpec(
            (DEVICES // SERVE_STEPS, CAP * PARTS, 128), lambda i: (i, 0, 0)
        ),
        compiler_params=params(),
        name="serve",
    )(asked, in_hbm(field))


def tables_kernel(
    seg_ref, coords_ref, weights_ref, high_ref, rest_ref, modes, slave_tab, master_tab
):
    step = pl.program_id(0)
    points = weights_ref.shape[1]
    row = lax.broadcasted_iota(jnp.int32, (PAIR_BLOCK, points), 0)
    point = lax.broadcasted_iota(jnp.int32, (PAIR_BLOCK, points), 1)
    used = jnp.zeros((PAIR_BLOCK, points), jnp.int32)
    for p in range(PAIR_BLOCK):
        used = jnp.where(row == p, seg_ref[step * PAIR_BLOCK + p] * QPTS, used)
    weights = jnp.where(point < used, weights_ref[...], 0.0)
    for k in range(4):
        x = coords_ref[:, k, :]
        now = weights if k == 0 else jnp.ones_like(x)
        later = now * x
        twice = x + x
        for n in range(MODES):
            modes[k, :, n, :] = now
            now, later = later, twice * later - now

    def build(p):
        for table, along, across in ((master_tab, 2, 3), (slave_tab, 0, 1)):
            inner = modes[across, p]
            for a in range(MODES):
                outer = modes[along, p, a : a + 1, :]
                table[p, a * MODES : (a + 1) * MODES, :] = (inner * outer).astype(bf16)

    def emit(p):
        turned = lax.dot_general(
            master_tab[p], slave_tab[p], (((1,), (1,)), ((), ())), preferred_element_type=f32
        )
        high = turned.astype(bf16)
        high_ref[p] = high
        rest_ref[p] = ((turned - high.astype(f32)) * REST_SCALE).astype(f8)

    build(0)
    for p in range(PAIR_BLOCK):
        if p + 1 < PAIR_BLOCK:
            build(p + 1)
        emit(p)


def couple_tables(seg_count, coords, weights):
    points = weights.shape[1]
    block = pl.BlockSpec((PAIR_BLOCK, NODES, NODES), lambda i, *_: (i, 0, 0))
    return pl.pallas_call(
        tables_kernel,
        grid_spec=pltpu.PrefetchScalarGridSpec(
            num_scalar_prefetch=1,
            grid=(PAIRS // PAIR_BLOCK,),
            in_specs=[
                pl.BlockSpec((PAIR_BLOCK, 4, points), lambda i, *_: (i, 0, 0)),
                pl.BlockSpec((PAIR_BLOCK, points), lambda i, *_: (i, 0)),
            ],
            out_specs=[block, block],
            scratch_shapes=[
                pltpu.VMEM((4, PAIR_BLOCK, MODES, points), f32),
                pltpu.VMEM((PAIR_BLOCK, NODES, points), bf16),
                pltpu.VMEM((PAIR_BLOCK, NODES, points), bf16),
            ],
        ),
        out_shape=[
            pltpu.HBM((PAIRS, NODES, NODES), bf16),
            pltpu.HBM((PAIRS, NODES, NODES), f8),
        ],
        compiler_params=pltpu.CompilerParams(vmem_limit_bytes=32 << 20),
        cost_estimate=pl.CostEstimate(
            flops=8 * PAIRS * NODES * NODES * points, bytes_accessed=64 << 20, transcendentals=0
        ),
        name="couple_tables",
    )(seg_count, in_hbm(coords), in_hbm(weights))


def two_pieces(u):
    high = u.astype(bf16)
    low = u - high.astype(f32)
    return jnp.concatenate([high.astype(f32), low], axis=0).astype(bf16)


def two_small_pieces(u):
    high = u.astype(f8).astype(f32)
    return jnp.concatenate([high, u - high, jnp.zeros((16, u.shape[1]), f32)], axis=0).astype(f8)


def times(pieces, table):
    both = lax.dot_general(pieces, table, (((1,), (0,)), ((), ())), preferred_element_type=f32)
    return both[0:8] + both[8:16]


def times_turned(pieces, table):
    both = lax.dot_general(table, pieces, (((1,), (1,)), ((), ())), preferred_element_type=f32)
    both = jnp.transpose(both)
    return both[0:8] + both[8:16]


COUPLE_BLOCK = 16
SLOTS = 4


def couple_kernel(
    slot_ref, row_ref, high_ref, rest_ref, field_ref, arrived_ref,
    gap_ref, back_ref, highs, rests, held, held_small, sems,
):
    count = PAIRS // COUPLE_BLOCK

    def copies(block):
        room = lax.rem(block, SLOTS)
        here = pl.ds(block * COUPLE_BLOCK, COUPLE_BLOCK)
        return (
            pltpu.make_async_copy(high_ref.at[here], highs.at[room], sems.at[0, room]),
            pltpu.make_async_copy(rest_ref.at[here], rests.at[room], sems.at[1, room]),
        )

    def start(block):
        for copy in copies(block):
            copy.start()

    def wait(block):
        for copy in copies(block):
            copy.wait()

    empty = jnp.zeros((5, NODES), f32)

    def pull(block, p):
        room = lax.rem(block, SLOTS)
        pair = block * COUPLE_BLOCK + p
        both = arrived_ref[pl.ds(slot_ref[pair] * PARTS, PARTS), :]
        u = jnp.concatenate([both[0:3], both[3:6]], axis=1)
        u = jnp.concatenate([u, empty], axis=0)
        pulled = times(two_pieces(u), highs[room, p])
        pulled = pulled + times(two_small_pieces(u), rests[room, p]) * (1.0 / REST_SCALE)
        r = row_ref[pair]
        lines = [field_ref[c, pl.ds(r, 1), :] for c in range(3)]
        gap = jnp.concatenate(lines + [empty], axis=0) - pulled
        for c in range(3):
            gap_ref[c, pl.ds(pair, 1), :] = gap[c : c + 1]
        half = PENALTY * gap
        held[p] = two_pieces(half)
        held_small[p] = two_small_pieces(half)

    def push(block, p):
        room = lax.rem(block, SLOTS)
        back = times_turned(held[p], highs[room, p])
        back = back + times_turned(held_small[p], rests[room, p]) * (1.0 / REST_SCALE)
        back_ref[pl.ds(slot_ref[block * COUPLE_BLOCK + p] * PARTS, PARTS), :] = jnp.concatenate(
            [back[0:3, 0:128], back[0:3, 128:256]], axis=0
        )

    for ahead in range(SLOTS - 1):
        start(ahead)
    back_ref[...] = jnp.zeros_like(back_ref)
    wait(0)
    for p in range(COUPLE_BLOCK):
        pull(0, p)

    def one(block, carry):
        wait(block)

        @pl.when(block + SLOTS - 2 < count)
        def _():
            start(block + SLOTS - 2)

        for p in range(COUPLE_BLOCK):
            push(block - 1, p)
            pull(block, p)
        return carry

    lax.fori_loop(1, count, one, 0)
    for p in range(COUPLE_BLOCK):
        push(count - 1, p)


def couple(slot, slave_row, turned, field, arrived):
    whole = lambda *_: (0, 0, 0)
    flat = pl.BlockSpec((SLOT_ROWS, 128), lambda *_: (0, 0))
    anywhere = pl.BlockSpec(memory_space=pl.ANY)
    return pl.pallas_call(
        couple_kernel,
        grid_spec=pltpu.PrefetchScalarGridSpec(
            num_scalar_prefetch=2,
            grid=(1,),
            in_specs=[anywhere, anywhere, pl.BlockSpec((3, ROWS, NODES), whole), vmem()],
            out_specs=[pl.BlockSpec((3, PAIRS, NODES), whole), flat],
            scratch_shapes=[
                pltpu.VMEM((SLOTS, COUPLE_BLOCK, NODES, NODES), bf16),
                pltpu.VMEM((SLOTS, COUPLE_BLOCK, NODES, NODES), f8),
                pltpu.VMEM((COUPLE_BLOCK, 16, NODES), bf16),
                pltpu.VMEM((COUPLE_BLOCK, 32, NODES), f8),
                pltpu.SemaphoreType.DMA((2, SLOTS)),
            ],
        ),
        out_shape=[
            pltpu.HBM((3, PAIRS, NODES), f32),
            pltpu.HBM((SLOT_ROWS, 128), f32),
        ],
        compiler_params=params(),
        name="couple",
    )(slot, slave_row, *turned, in_hbm(field), in_vmem(arrived))


def gathered(hits, lines):
    high = lines.astype(bf16)
    low = (lines - high.astype(f32)).astype(bf16)
    dims = (((1,), (0,)), ((), ()))
    return lax.dot_general(hits, high, dims, preferred_element_type=f32) + lax.dot_general(
        hits, low, dims, preferred_element_type=f32
    )


def turned_sides(inside_ref, left_ref, right_ref):
    count = left_ref.shape[0]
    pad = jnp.zeros((8 - count, ROWS), f32)
    left, right = left_ref[...] * inside_ref[2], right_ref[...] * inside_ref[3]
    x = jnp.concatenate([left, pad, right, pad], axis=0)
    high = x.astype(bf16).astype(f32)
    rest = x - high
    middle = rest.astype(bf16).astype(f32)
    pieces = jnp.concatenate([high, middle, rest - middle, jnp.zeros((80, ROWS), f32)], axis=0)
    return jnp.transpose(pieces).astype(bf16)


def beside(u, above, below, sides, c):
    row = lax.broadcasted_iota(jnp.int32, (ROWS, NODES), 0)
    col = lax.broadcasted_iota(jnp.int32, (ROWS, NODES), 1)
    up = jnp.where(row == 0, above, pltpu.roll(u, 1, 0))
    down = jnp.where(row == ROWS - 1, below, pltpu.roll(u, ROWS - 1, 0))
    west = jnp.where(col == 0, 0.0, pltpu.roll(u, 1, 1))
    east = jnp.where(col == NODES - 1, 0.0, pltpu.roll(u, NODES - 1, 1))
    piece = lax.broadcasted_iota(jnp.int32, (128, NODES), 0) & 15
    place = lax.broadcasted_iota(jnp.int32, (128, NODES), 1)
    pick = ((piece == c) & (place == 0)) | ((piece == 8 + c) & (place == NODES - 1))
    pick = jnp.where(pick, 1.0, 0.0).astype(bf16)
    rim = lax.dot_general(sides, pick, (((1,), (0,)), ((), ())), preferred_element_type=f32)
    return (down + up) + (east + west) + rim


def swept(u, right, gain, inside_ref, above_ref, below_ref, sides, c):
    above = above_ref[c : c + 1, :] * inside_ref[0]
    below = below_ref[c : c + 1, :] * inside_ref[1]
    around = beside(u, above, below, sides, c)
    return (1.0 - RELAX) * u + gain * (right + around)


def put_edges(c, u, edges):
    top, bottom, left, right = edges
    top[c : c + 1, :] = u[0:1]
    bottom[c : c + 1, :] = u[ROWS - 1 : ROWS]
    left[c : c + 1, :] = jnp.transpose(u[:, 0:128])[0:1]
    right[c : c + 1, :] = jnp.transpose(u[:, 128:256])[127:128]


def slave_right_kernel(row_ref, gap_ref, load_ref, stiff_ref, right_out, gain_out):
    row = lax.broadcasted_iota(jnp.int32, (ROWS, PAIRS), 0)
    hits = jnp.where(row == row_ref[...], 1.0, 0.0).astype(bf16)
    gain_out[...] = RELAX / (4.0 + stiff_ref[...])
    for c in range(3):
        right_out[c] = load_ref[c] - PENALTY * gathered(hits, gap_ref[c])


def slave_right_side(slave_row, gap, load, stiffness):
    half = pl.BlockSpec((3, ROWS, NODES), lambda i: (0, 0, 0))
    plane = pl.BlockSpec((ROWS, NODES), lambda i: (0, 0))
    return pl.pallas_call(
        slave_right_kernel,
        grid=(1,),
        out_shape=[pltpu.HBM(FIELD.shape, f32), pltpu.HBM((ROWS, NODES), f32)],
        in_specs=[vmem(), pl.BlockSpec((3, PAIRS, NODES), lambda i: (0, 0, 0)), half, plane],
        out_specs=[half, plane],
        compiler_params=params(),
        name="slave_right_side",
    )(slave_row, in_hbm(gap), in_hbm(load), in_hbm(stiffness))


def early_sweep_kernel(
    inside_ref, u_ref, right_ref, load_ref, gain_ref, ha, hb, hl, hr, late_out, base_out, *edges
):
    gain = gain_ref[...]
    sides = turned_sides(inside_ref, hl, hr)
    for c in range(3):
        u = swept(u_ref[c], right_ref[c], gain, inside_ref, ha, hb, sides, c)
        late_out[c] = u
        late_out[3 + c] = right_ref[c]
        late_out[6 + c] = load_ref[c]
        put_edges(c, u, edges)
        base_out[c] = swept(u_ref[3 + c], load_ref[c], gain, inside_ref, ha, hb, sides, 3 + c)


def edges_kernel(u_ref, *edges):
    for c in range(6):
        put_edges(c, u_ref[c], edges)


def first_edges(displacement):
    return pl.pallas_call(
        edges_kernel,
        out_shape=[jax.ShapeDtypeStruct((6, 256), f32)] * 4,
        in_specs=[vmem()],
        out_specs=[vmem()] * 4,
        compiler_params=params(),
        name="first_edges",
    )(displacement)


EDGES = [jax.ShapeDtypeStruct((3, 256), f32)] * 4
FIELD = jax.ShapeDtypeStruct((3, ROWS, NODES), f32)


def early_sweep(within, displacement, right, load, gain, halos):
    part = pl.BlockSpec((3, ROWS, NODES), lambda i: (0, 0, 0))
    return pl.pallas_call(
        early_sweep_kernel,
        grid=(1,),
        out_shape=[pltpu.HBM((9, ROWS, NODES), f32), pltpu.HBM(FIELD.shape, f32)] + EDGES,
        in_specs=[
            smem(),
            vmem(),
            part,
            pl.BlockSpec((3, ROWS, NODES), lambda i: (1, 0, 0)),
            pl.BlockSpec((ROWS, NODES), lambda i: (0, 0)),
        ]
        + [vmem()] * 4,
        out_specs=[pl.BlockSpec((9, ROWS, NODES), lambda i: (0, 0, 0)), part] + [vmem()] * 4,
        compiler_params=params(),
        name="early_sweep",
    )(within, displacement, in_hbm(right), in_hbm(load), in_hbm(gain), *halos)


def master_sweep_kernel(
    asked_ref, incoming_ref, base_ref, gain_ref, ea, eb, el, er, u_out, added_out, *edges
):
    asked = jnp.transpose(asked_ref[...].reshape(DEVICES, 128))
    row = lax.broadcasted_iota(jnp.int32, (ROWS, DEVICES), 0)
    hits = jnp.concatenate(
        [jnp.where(row == asked[k : k + 1], 1.0, 0.0) for k in range(CAP)], axis=1
    ).astype(bf16)

    def force(part):
        lines = jnp.concatenate(
            [
                incoming_ref[pl.ds(k * PARTS + part, DEVICES, stride=CAP * PARTS), :]
                for k in range(CAP)
            ],
            axis=0,
        )
        return gathered(hits, lines)

    for edge, slave_edge in zip(edges, (ea, eb, el, er)):
        edge[0:3, :] = slave_edge[...]
    for c in range(3):
        added = jnp.concatenate([force(c), force(3 + c)], axis=1)
        added_out[c] = added
        u = base_ref[c] + gain_ref[...] * added
        u_out[c] = u
        put_edges(3 + c, u, edges)


def master_sweep(asked, incoming, base, gain, slave_edges):
    return pl.pallas_call(
        master_sweep_kernel,
        grid=(1,),
        out_shape=[FIELD, FIELD] + [jax.ShapeDtypeStruct((6, 256), f32)] * 4,
        in_specs=[
            vmem(),
            vmem(),
            pl.BlockSpec((3, ROWS, NODES), lambda i: (0, 0, 0)),
            pl.BlockSpec((ROWS, NODES), lambda i: (0, 0)),
        ]
        + [vmem()] * 4,
        out_specs=[vmem()] * 6,
        compiler_params=params(),
        name="master_sweep",
    )(asked, in_vmem(incoming), in_hbm(base), in_hbm(gain), *slave_edges)


def last_sweep_kernel(
    inside_ref, late_ref, um_ref, added_ref, gain_ref, ha, hb, hl, hr, out_ref, done, sems
):
    copies = []
    gain = gain_ref[...]
    sides = turned_sides(inside_ref, hl, hr)
    for c in range(6):
        if c < 3:
            u, right = late_ref[c], late_ref[3 + c]
        else:
            u, right = um_ref[c - 3], late_ref[3 + c] + added_ref[c - 3]
        done[c] = swept(u, right, gain, inside_ref, ha, hb, sides, c)
        copies.append(pltpu.make_async_copy(done.at[c], out_ref.at[c], sems.at[c]))
        copies[-1].start()
    for copy in copies:
        copy.wait()


def last_sweep(within, late, master_u, added, gain, halos):
    return pl.pallas_call(
        last_sweep_kernel,
        out_shape=jax.ShapeDtypeStruct((6, ROWS, NODES), f32),
        in_specs=[smem()] + [vmem()] * 8,
        out_specs=pl.BlockSpec(memory_space=pl.ANY),
        scratch_shapes=[pltpu.VMEM((6, ROWS, NODES), f32), pltpu.SemaphoreType.DMA((6,))],
        compiler_params=params(),
        name="last_sweep",
    )(within, late, master_u, added, gain, *halos)


def exchange(top, bottom, left, right):
    slabs, faces = lax.axis_size("slab"), lax.axis_size("face")
    onward = lambda n: [(i, (i + 1) % n) for i in range(n)]
    back = lambda n: [((i + 1) % n, i) for i in range(n)]
    return (
        lax.ppermute(bottom, "slab", onward(slabs)),
        lax.ppermute(top, "slab", back(slabs)),
        lax.ppermute(right, "face", onward(faces)),
        lax.ppermute(left, "face", back(faces)),
    )


def inside():
    slab, face = lax.axis_index("slab"), lax.axis_index("face")
    return jnp.stack(
        [slab > 0, slab < lax.axis_size("slab") - 1, face > 0, face < lax.axis_size("face") - 1]
    ).astype(f32)


def all_to_all(x):
    return lax.all_to_all(x, AXES, split_axis=0, concat_axis=0, tiled=True)


def body(
    displacement,
    load,
    stiffness,
    slave_row,
    master_dev,
    master_row,
    seg_count,
    quad_coords,
    quad_weights,
):
    request, slot = slots(master_dev.reshape(1, PAIRS), master_row.reshape(1, PAIRS))
    slot = slot.reshape(PAIRS)
    asked = all_to_all(request)
    first_halos = exchange(*first_edges(displacement))
    turned = couple_tables(seg_count, quad_coords, quad_weights)
    served = serve(asked.reshape(DEVICES * 128), displacement)
    arrived = all_to_all(served).reshape(SLOT_ROWS, 128)
    gap, outgoing = couple(slot, slave_row, turned, displacement, arrived)
    incoming = all_to_all(outgoing.reshape(DEVICES, CAP * PARTS, 128)).reshape(SLOT_ROWS, 128)
    slave_right, gain = slave_right_side(slave_row.reshape(1, PAIRS), gap, load, stiffness)
    within = inside()
    late, base, *slave_edges = early_sweep(
        within, displacement, slave_right, load, gain, first_halos
    )
    master_u, added, *edges = master_sweep(asked, incoming, base, gain, slave_edges)
    relaxed = last_sweep(within, late, master_u, added, gain, exchange(*edges))
    return relaxed, gap.transpose(1, 0, 2)


def solution(mesh):
    pairs = P(AXES)
    field = P(None, "slab", "face")
    return jax.shard_map(
        body,
        mesh=mesh,
        in_specs=(
            field,
            field,
            P("slab", "face"),
            pairs,
            P(AXES, None),
            pairs,
            pairs,
            P(AXES, None, None),
            P(AXES, None),
        ),
        out_specs=(field, P(AXES, None, None)),
        check_vma=False,
    )
```

```python
import functools

import jax
import jax.numpy as jnp
from jax import lax
from jax.experimental import pallas as pl
from jax.experimental.pallas import tpu as pltpu
from jax.sharding import PartitionSpec as P

MODES = 16
QPTS = 16
CAP = 4
PENALTY = 0.5
RELAX = 0.8
DEVICES = 128
PAIRS = 128
NODES = 256
ROWS = 256
PARTS = 6
SLOT_ROWS = DEVICES * CAP * PARTS
PAIR_BLOCK = 8

f32 = jnp.float32
bf16 = jnp.bfloat16
f8 = jnp.float8_e5m2
REST_SCALE = 4096.0
AXES = ("slab", "face")


def vmem():
    return pl.BlockSpec(memory_space=pltpu.VMEM)


def smem():
    return pl.BlockSpec(memory_space=pltpu.SMEM)


def in_vmem(x):
    return pltpu.with_memory_space_constraint(x, pltpu.VMEM)


def in_hbm(x):
    return pltpu.with_memory_space_constraint(x, pltpu.HBM)


def params():
    return pltpu.CompilerParams(vmem_limit_bytes=48 << 20)


def slots_kernel(dev_ref, row_ref, request_ref, slot_ref):
    dev = dev_ref[...]
    row = row_ref[...]
    spread = jnp.broadcast_to(dev, (PAIRS, PAIRS))
    across = jnp.transpose(spread)
    first = lax.broadcasted_iota(jnp.int32, (PAIRS, PAIRS), 0)
    second = lax.broadcasted_iota(jnp.int32, (PAIRS, PAIRS), 1)
    same = jnp.where((spread == across) & (first < second), 1.0, 0.0)
    rank = jnp.sum(same, axis=0, keepdims=True).astype(jnp.int32)
    slot_ref[...] = dev * CAP + rank
    hits = spread == first
    result = jnp.zeros((DEVICES, 128), jnp.int32)
    for k in range(CAP):
        chosen = jnp.where(hits & (rank == k), row.astype(f32), 0.0)
        found = jnp.sum(chosen, axis=1, keepdims=True).astype(jnp.int32)
        result = jnp.where(second == k, found, result)
    request_ref[...] = result.reshape(DEVICES, 1, 128)


def slots(dev, row):
    return pl.pallas_call(
        slots_kernel,
        out_shape=[
            jax.ShapeDtypeStruct((DEVICES, 1, 128), jnp.int32),
            jax.ShapeDtypeStruct((1, PAIRS), jnp.int32),
        ],
        in_specs=[vmem(), vmem()],
        out_specs=[vmem(), vmem()],
        name="slots",
    )(dev, row)


SERVE_STEPS = 2


def serve_kernel(asked_ref, field_ref, out_ref):
    begin = pl.program_id(0) * (DEVICES // SERVE_STEPS)

    def one(s, carry):
        lines = []
        for k in range(CAP):
            r = asked_ref[(begin + s) * 128 + k]
            lines.append([field_ref[c, pl.ds(r, 1), :] for c in range(3)])
        out_ref[s] = jnp.concatenate(
            [
                line[:, h * 128 : h * 128 + 128]
                for k in range(CAP)
                for h in range(2)
                for line in lines[k]
            ],
            axis=0,
        )
        return carry

    lax.fori_loop(0, DEVICES // SERVE_STEPS, one, 0, unroll=8)


def serve(asked, field):
    return pl.pallas_call(
        serve_kernel,
        grid=(SERVE_STEPS,),
        out_shape=pltpu.HBM((DEVICES, CAP * PARTS, 128), f32),
        in_specs=[smem(), pl.BlockSpec((3, ROWS, NODES), lambda i: (1, 0, 0))],
        out_specs=pl.BlockSpec(
            (DEVICES // SERVE_STEPS, CAP * PARTS, 128), lambda i: (i, 0, 0)
        ),
        compiler_params=params(),
        name="serve",
    )(asked, in_hbm(field))


def tables_kernel(
    seg_ref, coords_ref, weights_ref, high_ref, rest_ref, modes, slave_tab, master_tab
):
    step = pl.program_id(0)
    points = weights_ref.shape[1]
    row = lax.broadcasted_iota(jnp.int32, (PAIR_BLOCK, points), 0)
    point = lax.broadcasted_iota(jnp.int32, (PAIR_BLOCK, points), 1)
    used = jnp.zeros((PAIR_BLOCK, points), jnp.int32)
    for p in range(PAIR_BLOCK):
        used = jnp.where(row == p, seg_ref[step * PAIR_BLOCK + p] * QPTS, used)
    weights = jnp.where(point < used, weights_ref[...], 0.0)
    for k in range(4):
        x = coords_ref[:, k, :]
        now = weights if k == 0 else jnp.ones_like(x)
        later = now * x
        twice = x + x
        for n in range(MODES):
            modes[k, :, n, :] = now
            now, later = later, twice * later - now

    def build(p):
        for table, along, across in ((master_tab, 2, 3), (slave_tab, 0, 1)):
            inner = modes[across, p]
            for a in range(MODES):
                outer = modes[along, p, a : a + 1, :]
                table[p, a * MODES : (a + 1) * MODES, :] = (inner * outer).astype(bf16)

    def emit(p):
        turned = lax.dot_general(
            master_tab[p], slave_tab[p], (((1,), (1,)), ((), ())), preferred_element_type=f32
        )
        high = turned.astype(bf16)
        high_ref[p] = high
        rest_ref[p] = ((turned - high.astype(f32)) * REST_SCALE).astype(f8)

    build(0)
    for p in range(PAIR_BLOCK):
        if p + 1 < PAIR_BLOCK:
            build(p + 1)
        emit(p)


def couple_tables(seg_count, coords, weights):
    points = weights.shape[1]
    block = pl.BlockSpec((PAIR_BLOCK, NODES, NODES), lambda i, *_: (i, 0, 0))
    return pl.pallas_call(
        tables_kernel,
        grid_spec=pltpu.PrefetchScalarGridSpec(
            num_scalar_prefetch=1,
            grid=(PAIRS // PAIR_BLOCK,),
            in_specs=[
                pl.BlockSpec((PAIR_BLOCK, 4, points), lambda i, *_: (i, 0, 0)),
                pl.BlockSpec((PAIR_BLOCK, points), lambda i, *_: (i, 0)),
            ],
            out_specs=[block, block],
            scratch_shapes=[
                pltpu.VMEM((4, PAIR_BLOCK, MODES, points), f32),
                pltpu.VMEM((PAIR_BLOCK, NODES, points), bf16),
                pltpu.VMEM((PAIR_BLOCK, NODES, points), bf16),
            ],
        ),
        out_shape=[
            pltpu.HBM((PAIRS, NODES, NODES), bf16),
            pltpu.HBM((PAIRS, NODES, NODES), f8),
        ],
        compiler_params=pltpu.CompilerParams(vmem_limit_bytes=32 << 20),
        cost_estimate=pl.CostEstimate(
            flops=8 * PAIRS * NODES * NODES * points, bytes_accessed=64 << 20, transcendentals=0
        ),
        name="couple_tables",
    )(seg_count, in_hbm(coords), in_hbm(weights))


def two_pieces(u):
    high = u.astype(bf16)
    low = u - high.astype(f32)
    return jnp.concatenate([high.astype(f32), low], axis=0).astype(bf16)


def two_small_pieces(u):
    high = u.astype(f8).astype(f32)
    return jnp.concatenate([high, u - high, jnp.zeros((16, u.shape[1]), f32)], axis=0).astype(f8)


def times(pieces, table):
    both = lax.dot_general(pieces, table, (((1,), (0,)), ((), ())), preferred_element_type=f32)
    return both[0:8] + both[8:16]


def times_turned(pieces, table):
    both = lax.dot_general(table, pieces, (((1,), (1,)), ((), ())), preferred_element_type=f32)
    both = jnp.transpose(both)
    return both[0:8] + both[8:16]


COUPLE_BLOCK = 16
SLOTS = 4


def couple_kernel(
    slot_ref, row_ref, high_ref, rest_ref, field_ref, arrived_ref,
    gap_ref, back_ref, highs, rests, held, held_small, sems,
):
    count = PAIRS // COUPLE_BLOCK

    def copies(block):
        room = lax.rem(block, SLOTS)
        here = pl.ds(block * COUPLE_BLOCK, COUPLE_BLOCK)
        return (
            pltpu.make_async_copy(high_ref.at[here], highs.at[room], sems.at[0, room]),
            pltpu.make_async_copy(rest_ref.at[here], rests.at[room], sems.at[1, room]),
        )

    def start(block):
        for copy in copies(block):
            copy.start()

    def wait(block):
        for copy in copies(block):
            copy.wait()

    empty = jnp.zeros((5, NODES), f32)

    def pull(block, p):
        room = lax.rem(block, SLOTS)
        pair = block * COUPLE_BLOCK + p
        both = arrived_ref[pl.ds(slot_ref[pair] * PARTS, PARTS), :]
        u = jnp.concatenate([both[0:3], both[3:6]], axis=1)
        u = jnp.concatenate([u, empty], axis=0)
        pulled = times(two_pieces(u), highs[room, p])
        pulled = pulled + times(two_small_pieces(u), rests[room, p]) * (1.0 / REST_SCALE)
        r = row_ref[pair]
        lines = [field_ref[c, pl.ds(r, 1), :] for c in range(3)]
        gap = jnp.concatenate(lines + [empty], axis=0) - pulled
        for c in range(3):
            gap_ref[c, pl.ds(pair, 1), :] = gap[c : c + 1]
        half = PENALTY * gap
        held[p] = two_pieces(half)
        held_small[p] = two_small_pieces(half)

    def push(block, p):
        room = lax.rem(block, SLOTS)
        back = times_turned(held[p], highs[room, p])
        back = back + times_turned(held_small[p], rests[room, p]) * (1.0 / REST_SCALE)
        back_ref[pl.ds(slot_ref[block * COUPLE_BLOCK + p] * PARTS, PARTS), :] = jnp.concatenate(
            [back[0:3, 0:128], back[0:3, 128:256]], axis=0
        )

    for ahead in range(SLOTS - 1):
        start(ahead)
    back_ref[...] = jnp.zeros_like(back_ref)
    wait(0)
    for p in range(COUPLE_BLOCK):
        pull(0, p)

    def one(block, carry):
        wait(block)

        @pl.when(block + SLOTS - 2 < count)
        def _():
            start(block + SLOTS - 2)

        for p in range(COUPLE_BLOCK):
            push(block - 1, p)
            pull(block, p)
        return carry

    lax.fori_loop(1, count, one, 0)
    for p in range(COUPLE_BLOCK):
        push(count - 1, p)


def couple(slot, slave_row, turned, field, arrived):
    whole = lambda *_: (0, 0, 0)
    flat = pl.BlockSpec((SLOT_ROWS, 128), lambda *_: (0, 0))
    anywhere = pl.BlockSpec(memory_space=pl.ANY)
    return pl.pallas_call(
        couple_kernel,
        grid_spec=pltpu.PrefetchScalarGridSpec(
            num_scalar_prefetch=2,
            grid=(1,),
            in_specs=[anywhere, anywhere, pl.BlockSpec((3, ROWS, NODES), whole), vmem()],
            out_specs=[pl.BlockSpec((3, PAIRS, NODES), whole), flat],
            scratch_shapes=[
                pltpu.VMEM((SLOTS, COUPLE_BLOCK, NODES, NODES), bf16),
                pltpu.VMEM((SLOTS, COUPLE_BLOCK, NODES, NODES), f8),
                pltpu.VMEM((COUPLE_BLOCK, 16, NODES), bf16),
                pltpu.VMEM((COUPLE_BLOCK, 32, NODES), f8),
                pltpu.SemaphoreType.DMA((2, SLOTS)),
            ],
        ),
        out_shape=[
            pltpu.HBM((3, PAIRS, NODES), f32),
            pltpu.HBM((SLOT_ROWS, 128), f32),
        ],
        compiler_params=params(),
        name="couple",
    )(slot, slave_row, *turned, in_hbm(field), in_vmem(arrived))


def gathered(hits, lines):
    high = lines.astype(bf16)
    low = (lines - high.astype(f32)).astype(bf16)
    dims = (((1,), (0,)), ((), ()))
    return lax.dot_general(hits, high, dims, preferred_element_type=f32) + lax.dot_general(
        hits, low, dims, preferred_element_type=f32
    )


def inside():
    slab, face = lax.axis_index("slab"), lax.axis_index("face")
    there = [slab > 0, slab < lax.axis_size("slab") - 1, face > 0, face < lax.axis_size("face") - 1]
    return [jnp.where(neighbour, 1.0, 0.0) for neighbour in there]


def turned_sides(within, left_ref, right_ref):
    count = left_ref.shape[0]
    pad = jnp.zeros((8 - count, ROWS), f32)
    left, right = left_ref[...] * within[2], right_ref[...] * within[3]
    x = jnp.concatenate([left, pad, right, pad], axis=0)
    high = x.astype(bf16).astype(f32)
    rest = x - high
    middle = rest.astype(bf16).astype(f32)
    pieces = jnp.concatenate([high, middle, rest - middle, jnp.zeros((80, ROWS), f32)], axis=0)
    return jnp.transpose(pieces).astype(bf16)


def inner(u):
    row = lax.broadcasted_iota(jnp.int32, (ROWS, NODES), 0)
    col = lax.broadcasted_iota(jnp.int32, (ROWS, NODES), 1)
    up = jnp.where(row == 0, 0.0, pltpu.roll(u, 1, 0))
    down = jnp.where(row == ROWS - 1, 0.0, pltpu.roll(u, ROWS - 1, 0))
    west = jnp.where(col == 0, 0.0, pltpu.roll(u, 1, 1))
    east = jnp.where(col == NODES - 1, 0.0, pltpu.roll(u, NODES - 1, 1))
    return (down + up) + (east + west)


def rim(within, above_ref, below_ref, sides, c):
    row = lax.broadcasted_iota(jnp.int32, (ROWS, NODES), 0)
    piece = lax.broadcasted_iota(jnp.int32, (128, NODES), 0) & 15
    place = lax.broadcasted_iota(jnp.int32, (128, NODES), 1)
    pick = ((piece == c) & (place == 0)) | ((piece == 8 + c) & (place == NODES - 1))
    pick = jnp.where(pick, 1.0, 0.0).astype(bf16)
    beside = lax.dot_general(sides, pick, (((1,), (0,)), ((), ())), preferred_element_type=f32)
    above = above_ref[c : c + 1, :] * within[0]
    below = below_ref[c : c + 1, :] * within[1]
    return beside + jnp.where(row == 0, above, jnp.where(row == ROWS - 1, below, 0.0))


def swept(u, right, gain, around):
    return (1.0 - RELAX) * u + gain * (right + around)


def put_edges(c, u, edges):
    top, bottom, left, right = edges
    top[c : c + 1, :] = u[0:1]
    bottom[c : c + 1, :] = u[ROWS - 1 : ROWS]
    left[c : c + 1, :] = jnp.transpose(u[:, 0:128])[0:1]
    right[c : c + 1, :] = jnp.transpose(u[:, 128:256])[127:128]


def early_sweep_kernel(row_ref, gap_ref, u_ref, load_ref, stiff_ref, right_out, first_out, gain_out):
    row = lax.broadcasted_iota(jnp.int32, (ROWS, PAIRS), 0)
    hits = jnp.where(row == row_ref[...], 1.0, 0.0).astype(bf16)
    gain = RELAX / (4.0 + stiff_ref[...])
    gain_out[...] = gain
    for c in range(6):
        right = load_ref[c]
        if c < 3:
            right = right - PENALTY * gathered(hits, gap_ref[c])
        right_out[c] = right
        first_out[c] = swept(u_ref[c], right, gain, inner(u_ref[c]))


def early_sweep(slave_row, gap, displacement, load, stiffness):
    whole = pl.BlockSpec((6, ROWS, NODES), lambda i: (0, 0, 0))
    plane = pl.BlockSpec((ROWS, NODES), lambda i: (0, 0))
    field = pltpu.HBM((6, ROWS, NODES), f32)
    return pl.pallas_call(
        early_sweep_kernel,
        grid=(1,),
        out_shape=[field, field, pltpu.HBM((ROWS, NODES), f32)],
        in_specs=[
            vmem(), pl.BlockSpec((3, PAIRS, NODES), lambda i: (0, 0, 0)), whole, whole, plane
        ],
        out_specs=[whole, whole, plane],
        compiler_params=params(),
        name="early_sweep",
    )(slave_row, in_hbm(gap), in_hbm(displacement), in_hbm(load), in_hbm(stiffness))


def edges_kernel(u_ref, *edges):
    for c in range(6):
        put_edges(c, u_ref[c], edges)


def first_edges(displacement):
    return pl.pallas_call(
        edges_kernel,
        out_shape=[jax.ShapeDtypeStruct((6, 256), f32)] * 4,
        in_specs=[vmem()],
        out_specs=[vmem()] * 4,
        compiler_params=params(),
        name="first_edges",
    )(displacement)


def master_sweep_kernel(
    asked_ref, incoming_ref, first_ref, gain_ref, ha, hb, hl, hr,
    u_out, added_out, *refs
):
    edges, first, gain_here, sems = refs[:4], *refs[4:]
    within = inside()
    arrivals = [
        pltpu.make_async_copy(first_ref.at[c], first.at[c], sems.at[c]) for c in range(6)
    ]
    arrivals.append(pltpu.make_async_copy(gain_ref, gain_here, sems.at[6]))
    for k in (6, 3, 4, 5, 0, 1, 2):
        arrivals[k].start()
    asked = jnp.transpose(asked_ref[...].reshape(DEVICES, 128))
    row = lax.broadcasted_iota(jnp.int32, (ROWS, DEVICES), 0)
    hits = jnp.concatenate(
        [jnp.where(row == asked[k : k + 1], 1.0, 0.0) for k in range(CAP)], axis=1
    ).astype(bf16)

    def force(part):
        lines = jnp.concatenate(
            [
                incoming_ref[pl.ds(k * PARTS + part, DEVICES, stride=CAP * PARTS), :]
                for k in range(CAP)
            ],
            axis=0,
        )
        return gathered(hits, lines)

    sides = turned_sides(within, hl, hr)
    for c in (3, 4, 5, 0, 1, 2):
        more = rim(within, ha, hb, sides, c)
        if c >= 3:
            added = jnp.concatenate([force(c - 3), force(c)], axis=1)
            added_out[c - 3] = added
            more = more + added
        if c == 3:
            arrivals[6].wait()
        arrivals[c].wait()
        u = first[c] + gain_here[...] * more
        u_out[c] = u
        put_edges(c, u, edges)


def master_sweep(asked, incoming, first, gain, halos):
    lines = jax.ShapeDtypeStruct((6, 256), f32)
    return pl.pallas_call(
        master_sweep_kernel,
        out_shape=[jax.ShapeDtypeStruct((n, ROWS, NODES), f32) for n in (6, 3)] + [lines] * 4,
        in_specs=[
            vmem(),
            vmem(),
            pl.BlockSpec(memory_space=pl.ANY),
            pl.BlockSpec(memory_space=pl.ANY),
        ]
        + [vmem()] * 4,
        out_specs=[vmem()] * 6,
        scratch_shapes=[
            pltpu.VMEM((6, ROWS, NODES), f32),
            pltpu.VMEM((ROWS, NODES), f32),
            pltpu.SemaphoreType.DMA((7,)),
        ],
        compiler_params=params(),
        name="master_sweep",
    )(asked, in_vmem(incoming), in_hbm(first), in_hbm(gain), *halos)


def last_sweep_kernel(
    u_ref, right_ref, added_ref, gain_ref, ha, hb, hl, hr, out_ref, done, sems
):
    copies = []
    within = inside()
    gain = gain_ref[...]
    sides = turned_sides(within, hl, hr)
    for c in range(6):
        right = right_ref[c] if c < 3 else right_ref[c] + added_ref[c - 3]
        around = inner(u_ref[c]) + rim(within, ha, hb, sides, c)
        done[c] = swept(u_ref[c], right, gain, around)
        copies.append(pltpu.make_async_copy(done.at[c], out_ref.at[c], sems.at[c]))
        copies[-1].start()
    for copy in copies:
        copy.wait()


def last_sweep(u, right, added, gain, halos):
    return pl.pallas_call(
        last_sweep_kernel,
        out_shape=jax.ShapeDtypeStruct((6, ROWS, NODES), f32),
        in_specs=[vmem()] * 8,
        out_specs=pl.BlockSpec(memory_space=pl.ANY),
        scratch_shapes=[pltpu.VMEM((6, ROWS, NODES), f32), pltpu.SemaphoreType.DMA((6,))],
        compiler_params=params(),
        name="last_sweep",
    )(u, right, added, gain, *halos)


def exchange(top, bottom, left, right):
    slabs, faces = lax.axis_size("slab"), lax.axis_size("face")
    onward = lambda n: [(i, (i + 1) % n) for i in range(n)]
    back = lambda n: [((i + 1) % n, i) for i in range(n)]
    return (
        lax.ppermute(bottom, "slab", onward(slabs)),
        lax.ppermute(top, "slab", back(slabs)),
        lax.ppermute(right, "face", onward(faces)),
        lax.ppermute(left, "face", back(faces)),
    )


def all_to_all(x):
    return lax.all_to_all(x, AXES, split_axis=0, concat_axis=0, tiled=True)


def body(
    displacement,
    load,
    stiffness,
    slave_row,
    master_dev,
    master_row,
    seg_count,
    quad_coords,
    quad_weights,
):
    request, slot = slots(master_dev.reshape(1, PAIRS), master_row.reshape(1, PAIRS))
    slot = slot.reshape(PAIRS)
    asked = all_to_all(request)
    first_halos = exchange(*first_edges(displacement))
    turned = couple_tables(seg_count, quad_coords, quad_weights)
    served = serve(asked.reshape(DEVICES * 128), displacement)
    arrived = all_to_all(served).reshape(SLOT_ROWS, 128)
    gap, outgoing = couple(slot, slave_row, turned, displacement, arrived)
    incoming = all_to_all(outgoing.reshape(DEVICES, CAP * PARTS, 128)).reshape(SLOT_ROWS, 128)
    right, first, gain = early_sweep(
        slave_row.reshape(1, PAIRS), gap, displacement, load, stiffness
    )
    u, added, *edges = master_sweep(asked, incoming, first, gain, first_halos)
    relaxed = last_sweep(u, right, added, gain, exchange(*edges))
    return relaxed, gap.transpose(1, 0, 2)


def solution(mesh):
    pairs = P(AXES)
    field = P(None, "slab", "face")
    return jax.shard_map(
        body,
        mesh=mesh,
        in_specs=(
            field,
            field,
            P("slab", "face"),
            pairs,
            P(AXES, None),
            pairs,
            pairs,
            P(AXES, None, None),
            P(AXES, None),
        ),
        out_specs=(field, P(AXES, None, None)),
        check_vma=False,
    )
```

```python
import functools

import jax
import jax.numpy as jnp
from jax import lax
from jax.experimental import pallas as pl
from jax.experimental.pallas import tpu as pltpu
from jax.sharding import PartitionSpec as P

MODES = 16
QPTS = 16
CAP = 4
PENALTY = 0.5
RELAX = 0.8
DEVICES = 128
PAIRS = 128
NODES = 256
ROWS = 256
PARTS = 6
SLOT_ROWS = DEVICES * CAP * PARTS
PAIR_BLOCK = 8

f32 = jnp.float32
bf16 = jnp.bfloat16
f8 = jnp.float8_e5m2
REST_SCALE = 4096.0
AXES = ("slab", "face")


def vmem():
    return pl.BlockSpec(memory_space=pltpu.VMEM)


def smem():
    return pl.BlockSpec(memory_space=pltpu.SMEM)


def in_vmem(x):
    return pltpu.with_memory_space_constraint(x, pltpu.VMEM)


def in_hbm(x):
    return pltpu.with_memory_space_constraint(x, pltpu.HBM)


def params():
    return pltpu.CompilerParams(vmem_limit_bytes=48 << 20)


def slots_kernel(dev_ref, row_ref, request_ref, slot_ref):
    dev = dev_ref[...]
    row = row_ref[...]
    spread = jnp.broadcast_to(dev, (PAIRS, PAIRS))
    across = jnp.transpose(spread)
    first = lax.broadcasted_iota(jnp.int32, (PAIRS, PAIRS), 0)
    second = lax.broadcasted_iota(jnp.int32, (PAIRS, PAIRS), 1)
    same = jnp.where((spread == across) & (first < second), 1.0, 0.0)
    rank = jnp.sum(same, axis=0, keepdims=True).astype(jnp.int32)
    slot_ref[...] = dev * CAP + rank
    hits = spread == first
    result = jnp.zeros((DEVICES, 128), jnp.int32)
    for k in range(CAP):
        chosen = jnp.where(hits & (rank == k), row.astype(f32), 0.0)
        found = jnp.sum(chosen, axis=1, keepdims=True).astype(jnp.int32)
        result = jnp.where(second == k, found, result)
    request_ref[...] = result.reshape(DEVICES, 1, 128)


def slots(dev, row):
    return pl.pallas_call(
        slots_kernel,
        out_shape=[
            jax.ShapeDtypeStruct((DEVICES, 1, 128), jnp.int32),
            jax.ShapeDtypeStruct((1, PAIRS), jnp.int32),
        ],
        in_specs=[vmem(), vmem()],
        out_specs=[vmem(), vmem()],
        name="slots",
    )(dev, row)


SERVE_STEPS = 2


def serve_kernel(asked_ref, field_ref, out_ref):
    begin = pl.program_id(0) * (DEVICES // SERVE_STEPS)

    def one(s, carry):
        lines = []
        for k in range(CAP):
            r = asked_ref[(begin + s) * 128 + k]
            lines.append([field_ref[c, pl.ds(r, 1), :] for c in range(3)])
        out_ref[s] = jnp.concatenate(
            [
                line[:, h * 128 : h * 128 + 128]
                for k in range(CAP)
                for h in range(2)
                for line in lines[k]
            ],
            axis=0,
        )
        return carry

    lax.fori_loop(0, DEVICES // SERVE_STEPS, one, 0, unroll=8)


def serve(asked, field):
    return pl.pallas_call(
        serve_kernel,
        grid=(SERVE_STEPS,),
        out_shape=pltpu.HBM((DEVICES, CAP * PARTS, 128), f32),
        in_specs=[smem(), pl.BlockSpec((3, ROWS, NODES), lambda i: (1, 0, 0))],
        out_specs=pl.BlockSpec(
            (DEVICES // SERVE_STEPS, CAP * PARTS, 128), lambda i: (i, 0, 0)
        ),
        compiler_params=params(),
        name="serve",
    )(asked, in_hbm(field))


def tables_kernel(
    seg_ref, coords_ref, weights_ref, high_ref, rest_ref, modes, slave_tab, master_tab
):
    step = pl.program_id(0)
    points = weights_ref.shape[1]
    row = lax.broadcasted_iota(jnp.int32, (PAIR_BLOCK, points), 0)
    point = lax.broadcasted_iota(jnp.int32, (PAIR_BLOCK, points), 1)
    used = jnp.zeros((PAIR_BLOCK, points), jnp.int32)
    for p in range(PAIR_BLOCK):
        used = jnp.where(row == p, seg_ref[step * PAIR_BLOCK + p] * QPTS, used)
    weights = jnp.where(point < used, weights_ref[...], 0.0)
    for k in range(4):
        x = coords_ref[:, k, :]
        now = weights if k == 0 else jnp.ones_like(x)
        later = now * x
        twice = x + x
        for n in range(MODES):
            modes[k, :, n, :] = now
            now, later = later, twice * later - now

    def build(p):
        for table, along, across in ((master_tab, 2, 3), (slave_tab, 0, 1)):
            inner = modes[across, p]
            for a in range(MODES):
                outer = modes[along, p, a : a + 1, :]
                table[p, a * MODES : (a + 1) * MODES, :] = (inner * outer).astype(bf16)

    def emit(p):
        turned = lax.dot_general(
            master_tab[p], slave_tab[p], (((1,), (1,)), ((), ())), preferred_element_type=f32
        )
        high = turned.astype(bf16)
        high_ref[p] = high
        rest_ref[p] = ((turned - high.astype(f32)) * REST_SCALE).astype(f8)

    build(0)
    for p in range(PAIR_BLOCK):
        if p + 1 < PAIR_BLOCK:
            build(p + 1)
        emit(p)


def couple_tables(seg_count, coords, weights):
    points = weights.shape[1]
    block = pl.BlockSpec((PAIR_BLOCK, NODES, NODES), lambda i, *_: (i, 0, 0))
    return pl.pallas_call(
        tables_kernel,
        grid_spec=pltpu.PrefetchScalarGridSpec(
            num_scalar_prefetch=1,
            grid=(PAIRS // PAIR_BLOCK,),
            in_specs=[
                pl.BlockSpec((PAIR_BLOCK, 4, points), lambda i, *_: (i, 0, 0)),
                pl.BlockSpec((PAIR_BLOCK, points), lambda i, *_: (i, 0)),
            ],
            out_specs=[block, block],
            scratch_shapes=[
                pltpu.VMEM((4, PAIR_BLOCK, MODES, points), f32),
                pltpu.VMEM((PAIR_BLOCK, NODES, points), bf16),
                pltpu.VMEM((PAIR_BLOCK, NODES, points), bf16),
            ],
        ),
        out_shape=[
            pltpu.HBM((PAIRS, NODES, NODES), bf16),
            pltpu.HBM((PAIRS, NODES, NODES), f8),
        ],
        compiler_params=pltpu.CompilerParams(vmem_limit_bytes=32 << 20),
        cost_estimate=pl.CostEstimate(
            flops=8 * PAIRS * NODES * NODES * points, bytes_accessed=64 << 20, transcendentals=0
        ),
        name="couple_tables",
    )(seg_count, in_hbm(coords), in_hbm(weights))


def two_pieces(u):
    high = u.astype(bf16)
    low = u - high.astype(f32)
    return jnp.concatenate([high.astype(f32), low], axis=0).astype(bf16)


def two_small_pieces(u):
    high = u.astype(f8).astype(f32)
    return jnp.concatenate([high, u - high, jnp.zeros((16, u.shape[1]), f32)], axis=0).astype(f8)


def times(pieces, table):
    both = lax.dot_general(pieces, table, (((1,), (0,)), ((), ())), preferred_element_type=f32)
    return both[0:8] + both[8:16]


def times_turned(pieces, table):
    both = lax.dot_general(table, pieces, (((1,), (1,)), ((), ())), preferred_element_type=f32)
    both = jnp.transpose(both)
    return both[0:8] + both[8:16]


COUPLE_BLOCK = 16
SLOTS = 4


def couple_kernel(
    slot_ref, row_ref, high_ref, rest_ref, field_ref, arrived_ref,
    gap_ref, back_ref, highs, rests, held, held_small, field_here, sems, field_sem,
):
    count = PAIRS // COUPLE_BLOCK

    def copies(block):
        room = lax.rem(block, SLOTS)
        here = pl.ds(block * COUPLE_BLOCK, COUPLE_BLOCK)
        return (
            pltpu.make_async_copy(high_ref.at[here], highs.at[room], sems.at[0, room]),
            pltpu.make_async_copy(rest_ref.at[here], rests.at[room], sems.at[1, room]),
        )

    def start(block):
        for copy in copies(block):
            copy.start()

    def wait(block):
        for copy in copies(block):
            copy.wait()

    empty = jnp.zeros((5, NODES), f32)

    def pull(block, p):
        room = lax.rem(block, SLOTS)
        pair = block * COUPLE_BLOCK + p
        both = arrived_ref[pl.ds(slot_ref[pair] * PARTS, PARTS), :]
        u = jnp.concatenate([both[0:3], both[3:6]], axis=1)
        u = jnp.concatenate([u, empty], axis=0)
        pulled = times(two_pieces(u), highs[room, p])
        pulled = pulled + times(two_small_pieces(u), rests[room, p]) * (1.0 / REST_SCALE)
        r = row_ref[pair]
        lines = [field_here[c, pl.ds(r, 1), :] for c in range(3)]
        gap = jnp.concatenate(lines + [empty], axis=0) - pulled
        for c in range(3):
            gap_ref[c, pl.ds(pair, 1), :] = gap[c : c + 1]
        half = PENALTY * gap
        held[p] = two_pieces(half)
        held_small[p] = two_small_pieces(half)

    def push(block, p):
        room = lax.rem(block, SLOTS)
        back = times_turned(held[p], highs[room, p])
        back = back + times_turned(held_small[p], rests[room, p]) * (1.0 / REST_SCALE)
        back_ref[pl.ds(slot_ref[block * COUPLE_BLOCK + p] * PARTS, PARTS), :] = jnp.concatenate(
            [back[0:3, 0:128], back[0:3, 128:256]], axis=0
        )

    start(0)
    field = pltpu.make_async_copy(field_ref.at[0:3], field_here, field_sem)
    field.start()
    start(1)
    back_ref[...] = jnp.zeros_like(back_ref)
    wait(0)
    start(2)
    field.wait()
    for p in range(COUPLE_BLOCK):
        pull(0, p)

    def one(block, carry):
        wait(block)

        @pl.when(block + SLOTS - 2 < count)
        def _():
            start(block + SLOTS - 2)

        for p in range(COUPLE_BLOCK):
            push(block - 1, p)
            pull(block, p)
        return carry

    lax.fori_loop(1, count, one, 0)
    for p in range(COUPLE_BLOCK):
        push(count - 1, p)


def couple(slot, slave_row, turned, field, arrived):
    whole = lambda *_: (0, 0, 0)
    flat = pl.BlockSpec((SLOT_ROWS, 128), lambda *_: (0, 0))
    anywhere = pl.BlockSpec(memory_space=pl.ANY)
    return pl.pallas_call(
        couple_kernel,
        grid_spec=pltpu.PrefetchScalarGridSpec(
            num_scalar_prefetch=2,
            grid=(1,),
            in_specs=[anywhere, anywhere, anywhere, vmem()],
            out_specs=[pl.BlockSpec((3, PAIRS, NODES), whole), flat],
            scratch_shapes=[
                pltpu.VMEM((SLOTS, COUPLE_BLOCK, NODES, NODES), bf16),
                pltpu.VMEM((SLOTS, COUPLE_BLOCK, NODES, NODES), f8),
                pltpu.VMEM((COUPLE_BLOCK, 16, NODES), bf16),
                pltpu.VMEM((COUPLE_BLOCK, 32, NODES), f8),
                pltpu.VMEM((3, ROWS, NODES), f32),
                pltpu.SemaphoreType.DMA((2, SLOTS)),
                pltpu.SemaphoreType.DMA,
            ],
        ),
        out_shape=[
            pltpu.HBM((3, PAIRS, NODES), f32),
            pltpu.HBM((SLOT_ROWS, 128), f32),
        ],
        compiler_params=params(),
        name="couple",
    )(slot, slave_row, *turned, in_hbm(field), in_vmem(arrived))


def gathered(hits, lines):
    high = lines.astype(bf16)
    low = (lines - high.astype(f32)).astype(bf16)
    dims = (((1,), (0,)), ((), ()))
    return lax.dot_general(hits, high, dims, preferred_element_type=f32) + lax.dot_general(
        hits, low, dims, preferred_element_type=f32
    )


def inside():
    slab, face = lax.axis_index("slab"), lax.axis_index("face")
    there = [slab > 0, slab < lax.axis_size("slab") - 1, face > 0, face < lax.axis_size("face") - 1]
    return [jnp.where(neighbour, 1.0, 0.0) for neighbour in there]


def turned_sides(within, left_ref, right_ref):
    count = left_ref.shape[0]
    pad = jnp.zeros((8 - count, ROWS), f32)
    left, right = left_ref[...] * within[2], right_ref[...] * within[3]
    x = jnp.concatenate([left, pad, right, pad], axis=0)
    high = x.astype(bf16).astype(f32)
    rest = x - high
    middle = rest.astype(bf16).astype(f32)
    pieces = jnp.concatenate([high, middle, rest - middle, jnp.zeros((80, ROWS), f32)], axis=0)
    return jnp.transpose(pieces).astype(bf16)


def inner(u):
    row = lax.broadcasted_iota(jnp.int32, (ROWS, NODES), 0)
    col = lax.broadcasted_iota(jnp.int32, (ROWS, NODES), 1)
    up = jnp.where(row == 0, 0.0, pltpu.roll(u, 1, 0))
    down = jnp.where(row == ROWS - 1, 0.0, pltpu.roll(u, ROWS - 1, 0))
    west = jnp.where(col == 0, 0.0, pltpu.roll(u, 1, 1))
    east = jnp.where(col == NODES - 1, 0.0, pltpu.roll(u, NODES - 1, 1))
    return (down + up) + (east + west)


def rim(within, above_ref, below_ref, sides, c):
    row = lax.broadcasted_iota(jnp.int32, (ROWS, NODES), 0)
    piece = lax.broadcasted_iota(jnp.int32, (128, NODES), 0) & 15
    place = lax.broadcasted_iota(jnp.int32, (128, NODES), 1)
    pick = ((piece == c) & (place == 0)) | ((piece == 8 + c) & (place == NODES - 1))
    pick = jnp.where(pick, 1.0, 0.0).astype(bf16)
    beside = lax.dot_general(sides, pick, (((1,), (0,)), ((), ())), preferred_element_type=f32)
    above = above_ref[c : c + 1, :] * within[0]
    below = below_ref[c : c + 1, :] * within[1]
    return beside + jnp.where(row == 0, above, jnp.where(row == ROWS - 1, below, 0.0))


def swept(u, right, gain, around):
    return (1.0 - RELAX) * u + gain * (right + around)


def put_edges(c, u, edges):
    top, bottom, left, right = edges
    top[c : c + 1, :] = u[0:1]
    bottom[c : c + 1, :] = u[ROWS - 1 : ROWS]
    left[c : c + 1, :] = jnp.transpose(u[:, 0:128])[0:1]
    right[c : c + 1, :] = jnp.transpose(u[:, 128:256])[127:128]


def early_sweep_kernel(row_ref, gap_ref, u_ref, load_ref, stiff_ref, right_out, first_out, gain_out):
    row = lax.broadcasted_iota(jnp.int32, (ROWS, PAIRS), 0)
    hits = jnp.where(row == row_ref[...], 1.0, 0.0).astype(bf16)
    gain = RELAX / (4.0 + stiff_ref[...])
    gain_out[...] = gain
    for c in range(6):
        right = load_ref[c]
        if c < 3:
            right = right - PENALTY * gathered(hits, gap_ref[c])
        right_out[c] = right
        first_out[c] = swept(u_ref[c], right, gain, inner(u_ref[c]))


def early_sweep(slave_row, gap, displacement, load, stiffness):
    whole = pl.BlockSpec((6, ROWS, NODES), lambda i: (0, 0, 0))
    plane = pl.BlockSpec((ROWS, NODES), lambda i: (0, 0))
    field = pltpu.HBM((6, ROWS, NODES), f32)
    return pl.pallas_call(
        early_sweep_kernel,
        grid=(1,),
        out_shape=[field, field, pltpu.HBM((ROWS, NODES), f32)],
        in_specs=[
            vmem(), pl.BlockSpec((3, PAIRS, NODES), lambda i: (0, 0, 0)), whole, whole, plane
        ],
        out_specs=[whole, whole, plane],
        compiler_params=params(),
        name="early_sweep",
    )(slave_row, in_hbm(gap), in_hbm(displacement), in_hbm(load), in_hbm(stiffness))


def edges_kernel(u_ref, *edges):
    for c in range(6):
        put_edges(c, u_ref[c], edges)


def first_edges(displacement):
    return pl.pallas_call(
        edges_kernel,
        out_shape=[jax.ShapeDtypeStruct((6, 256), f32)] * 4,
        in_specs=[vmem()],
        out_specs=[vmem()] * 4,
        compiler_params=params(),
        name="first_edges",
    )(displacement)


def master_sweep_kernel(
    asked_ref, incoming_ref, first_ref, gain_ref, ha, hb, hl, hr,
    u_out, added_out, *refs
):
    edges, first, gain_here, sems = refs[:4], *refs[4:]
    within = inside()
    arrivals = [
        pltpu.make_async_copy(first_ref.at[c], first.at[c], sems.at[c]) for c in range(6)
    ]
    arrivals.append(pltpu.make_async_copy(gain_ref, gain_here, sems.at[6]))
    for k in (6, 3, 4, 5, 0, 1, 2):
        arrivals[k].start()
    asked = jnp.transpose(asked_ref[...].reshape(DEVICES, 128))
    row = lax.broadcasted_iota(jnp.int32, (ROWS, DEVICES), 0)
    hits = jnp.concatenate(
        [jnp.where(row == asked[k : k + 1], 1.0, 0.0) for k in range(CAP)], axis=1
    ).astype(bf16)

    def force(part):
        lines = jnp.concatenate(
            [
                incoming_ref[pl.ds(k * PARTS + part, DEVICES, stride=CAP * PARTS), :]
                for k in range(CAP)
            ],
            axis=0,
        )
        return gathered(hits, lines)

    sides = turned_sides(within, hl, hr)
    for c in (3, 4, 5, 0, 1, 2):
        more = rim(within, ha, hb, sides, c)
        if c >= 3:
            added = jnp.concatenate([force(c - 3), force(c)], axis=1)
            added_out[c - 3] = added
            more = more + added
        if c == 3:
            arrivals[6].wait()
        arrivals[c].wait()
        u = first[c] + gain_here[...] * more
        u_out[c] = u
        put_edges(c, u, edges)


def master_sweep(asked, incoming, first, gain, halos):
    lines = jax.ShapeDtypeStruct((6, 256), f32)
    return pl.pallas_call(
        master_sweep_kernel,
        out_shape=[jax.ShapeDtypeStruct((n, ROWS, NODES), f32) for n in (6, 3)] + [lines] * 4,
        in_specs=[
            vmem(),
            vmem(),
            pl.BlockSpec(memory_space=pl.ANY),
            pl.BlockSpec(memory_space=pl.ANY),
        ]
        + [vmem()] * 4,
        out_specs=[vmem()] * 6,
        scratch_shapes=[
            pltpu.VMEM((6, ROWS, NODES), f32),
            pltpu.VMEM((ROWS, NODES), f32),
            pltpu.SemaphoreType.DMA((7,)),
        ],
        compiler_params=params(),
        name="master_sweep",
    )(asked, in_vmem(incoming), in_hbm(first), in_hbm(gain), *halos)


def last_sweep_kernel(
    u_ref, right_ref, added_ref, gain_ref, ha, hb, hl, hr, out_ref, done, sems
):
    copies = []
    within = inside()
    gain = gain_ref[...]
    sides = turned_sides(within, hl, hr)
    for c in range(6):
        right = right_ref[c] if c < 3 else right_ref[c] + added_ref[c - 3]
        around = inner(u_ref[c]) + rim(within, ha, hb, sides, c)
        done[c] = swept(u_ref[c], right, gain, around)
        copies.append(pltpu.make_async_copy(done.at[c], out_ref.at[c], sems.at[c]))
        copies[-1].start()
    for copy in copies:
        copy.wait()


def last_sweep(u, right, added, gain, halos):
    return pl.pallas_call(
        last_sweep_kernel,
        out_shape=jax.ShapeDtypeStruct((6, ROWS, NODES), f32),
        in_specs=[vmem()] * 8,
        out_specs=pl.BlockSpec(memory_space=pl.ANY),
        scratch_shapes=[pltpu.VMEM((6, ROWS, NODES), f32), pltpu.SemaphoreType.DMA((6,))],
        compiler_params=params(),
        name="last_sweep",
    )(u, right, added, gain, *halos)


def exchange(top, bottom, left, right):
    slabs, faces = lax.axis_size("slab"), lax.axis_size("face")
    onward = lambda n: [(i, (i + 1) % n) for i in range(n)]
    back = lambda n: [((i + 1) % n, i) for i in range(n)]
    return (
        lax.ppermute(bottom, "slab", onward(slabs)),
        lax.ppermute(top, "slab", back(slabs)),
        lax.ppermute(right, "face", onward(faces)),
        lax.ppermute(left, "face", back(faces)),
    )


def all_to_all(x):
    return lax.all_to_all(x, AXES, split_axis=0, concat_axis=0, tiled=True)


def body(
    displacement,
    load,
    stiffness,
    slave_row,
    master_dev,
    master_row,
    seg_count,
    quad_coords,
    quad_weights,
):
    request, slot = slots(master_dev.reshape(1, PAIRS), master_row.reshape(1, PAIRS))
    slot = slot.reshape(PAIRS)
    asked = all_to_all(request)
    first_halos = exchange(*first_edges(displacement))
    turned = couple_tables(seg_count, quad_coords, quad_weights)
    served = serve(asked.reshape(DEVICES * 128), displacement)
    arrived = all_to_all(served).reshape(SLOT_ROWS, 128)
    gap, outgoing = couple(slot, slave_row, turned, displacement, arrived)
    incoming = all_to_all(outgoing.reshape(DEVICES, CAP * PARTS, 128)).reshape(SLOT_ROWS, 128)
    right, first, gain = early_sweep(
        slave_row.reshape(1, PAIRS), gap, displacement, load, stiffness
    )
    u, added, *edges = master_sweep(asked, incoming, first, gain, first_halos)
    relaxed = last_sweep(u, right, added, gain, exchange(*edges))
    return relaxed, gap.transpose(1, 0, 2)


def solution(mesh):
    pairs = P(AXES)
    field = P(None, "slab", "face")
    return jax.shard_map(
        body,
        mesh=mesh,
        in_specs=(
            field,
            field,
            P("slab", "face"),
            pairs,
            P(AXES, None),
            pairs,
            pairs,
            P(AXES, None, None),
            P(AXES, None),
        ),
        out_specs=(field, P(AXES, None, None)),
        check_vma=False,
    )
```

```python
import functools

import jax
import jax.numpy as jnp
from jax import lax
from jax.experimental import pallas as pl
from jax.experimental.pallas import tpu as pltpu
from jax.sharding import PartitionSpec as P

MODES = 16
QPTS = 16
CAP = 4
PENALTY = 0.5
RELAX = 0.8
DEVICES = 128
PAIRS = 128
NODES = 256
ROWS = 256
PARTS = 6
SLOT_ROWS = DEVICES * CAP * PARTS
PAIR_BLOCK = 8

f32 = jnp.float32
bf16 = jnp.bfloat16
f8 = jnp.float8_e5m2
REST_SCALE = 4096.0
AXES = ("slab", "face")


def vmem():
    return pl.BlockSpec(memory_space=pltpu.VMEM)


def smem():
    return pl.BlockSpec(memory_space=pltpu.SMEM)


def in_vmem(x):
    return pltpu.with_memory_space_constraint(x, pltpu.VMEM)


def in_hbm(x):
    return pltpu.with_memory_space_constraint(x, pltpu.HBM)


def params():
    return pltpu.CompilerParams(vmem_limit_bytes=48 << 20)


def slots_kernel(dev_ref, row_ref, request_ref, slot_ref):
    dev = dev_ref[...]
    row = row_ref[...]
    spread = jnp.broadcast_to(dev, (PAIRS, PAIRS))
    across = jnp.transpose(spread)
    first = lax.broadcasted_iota(jnp.int32, (PAIRS, PAIRS), 0)
    second = lax.broadcasted_iota(jnp.int32, (PAIRS, PAIRS), 1)
    same = jnp.where((spread == across) & (first < second), 1.0, 0.0)
    rank = jnp.sum(same, axis=0, keepdims=True).astype(jnp.int32)
    slot_ref[...] = dev * CAP + rank
    hits = spread == first
    result = jnp.zeros((DEVICES, 128), jnp.int32)
    for k in range(CAP):
        chosen = jnp.where(hits & (rank == k), row.astype(f32), 0.0)
        found = jnp.sum(chosen, axis=1, keepdims=True).astype(jnp.int32)
        result = jnp.where(second == k, found, result)
    request_ref[...] = result.reshape(DEVICES, 1, 128)


def slots(dev, row):
    return pl.pallas_call(
        slots_kernel,
        out_shape=[
            jax.ShapeDtypeStruct((DEVICES, 1, 128), jnp.int32),
            jax.ShapeDtypeStruct((1, PAIRS), jnp.int32),
        ],
        in_specs=[vmem(), vmem()],
        out_specs=[vmem(), vmem()],
        name="slots",
    )(dev, row)


SERVE_STEPS = 2


def serve_kernel(asked_ref, field_ref, out_ref):
    begin = pl.program_id(0) * (DEVICES // SERVE_STEPS)

    def one(s, carry):
        lines = []
        for k in range(CAP):
            r = asked_ref[(begin + s) * 128 + k]
            lines.append([field_ref[c, pl.ds(r, 1), :] for c in range(3)])
        out_ref[s] = jnp.concatenate(
            [
                line[:, h * 128 : h * 128 + 128]
                for k in range(CAP)
                for h in range(2)
                for line in lines[k]
            ],
            axis=0,
        )
        return carry

    lax.fori_loop(0, DEVICES // SERVE_STEPS, one, 0, unroll=8)


def serve(asked, field):
    return pl.pallas_call(
        serve_kernel,
        grid=(SERVE_STEPS,),
        out_shape=pltpu.HBM((DEVICES, CAP * PARTS, 128), f32),
        in_specs=[smem(), pl.BlockSpec((3, ROWS, NODES), lambda i: (1, 0, 0))],
        out_specs=pl.BlockSpec(
            (DEVICES // SERVE_STEPS, CAP * PARTS, 128), lambda i: (i, 0, 0)
        ),
        compiler_params=params(),
        name="serve",
    )(asked, in_hbm(field))


def tables_kernel(
    seg_ref, coords_ref, weights_ref, high_ref, rest_ref, modes, slave_tab, master_tab
):
    step = pl.program_id(0)
    points = weights_ref.shape[1]
    row = lax.broadcasted_iota(jnp.int32, (PAIR_BLOCK, points), 0)
    point = lax.broadcasted_iota(jnp.int32, (PAIR_BLOCK, points), 1)
    used = jnp.zeros((PAIR_BLOCK, points), jnp.int32)
    for p in range(PAIR_BLOCK):
        used = jnp.where(row == p, seg_ref[step * PAIR_BLOCK + p] * QPTS, used)
    weights = jnp.where(point < used, weights_ref[...], 0.0)
    for k in range(4):
        x = coords_ref[:, k, :]
        now = weights if k == 0 else jnp.ones_like(x)
        later = now * x
        twice = x + x
        for n in range(MODES):
            modes[k, :, n, :] = now
            now, later = later, twice * later - now

    def build(p):
        for table, along, across in ((master_tab, 2, 3), (slave_tab, 0, 1)):
            inner = modes[across, p]
            for a in range(MODES):
                outer = modes[along, p, a : a + 1, :]
                table[p, a * MODES : (a + 1) * MODES, :] = (inner * outer).astype(bf16)

    def emit(p):
        turned = lax.dot_general(
            master_tab[p], slave_tab[p], (((1,), (1,)), ((), ())), preferred_element_type=f32
        )
        high = turned.astype(bf16)
        high_ref[p] = high
        rest_ref[p] = ((turned - high.astype(f32)) * REST_SCALE).astype(f8)

    build(0)
    for p in range(PAIR_BLOCK):
        if p + 1 < PAIR_BLOCK:
            build(p + 1)
        emit(p)


def couple_tables(seg_count, coords, weights):
    points = weights.shape[1]
    block = pl.BlockSpec((PAIR_BLOCK, NODES, NODES), lambda i, *_: (i, 0, 0))
    return pl.pallas_call(
        tables_kernel,
        grid_spec=pltpu.PrefetchScalarGridSpec(
            num_scalar_prefetch=1,
            grid=(PAIRS // PAIR_BLOCK,),
            in_specs=[
                pl.BlockSpec((PAIR_BLOCK, 4, points), lambda i, *_: (i, 0, 0)),
                pl.BlockSpec((PAIR_BLOCK, points), lambda i, *_: (i, 0)),
            ],
            out_specs=[block, block],
            scratch_shapes=[
                pltpu.VMEM((4, PAIR_BLOCK, MODES, points), f32),
                pltpu.VMEM((PAIR_BLOCK, NODES, points), bf16),
                pltpu.VMEM((PAIR_BLOCK, NODES, points), bf16),
            ],
        ),
        out_shape=[
            pltpu.HBM((PAIRS, NODES, NODES), bf16),
            pltpu.HBM((PAIRS, NODES, NODES), f8),
        ],
        compiler_params=pltpu.CompilerParams(vmem_limit_bytes=32 << 20),
        cost_estimate=pl.CostEstimate(
            flops=8 * PAIRS * NODES * NODES * points, bytes_accessed=64 << 20, transcendentals=0
        ),
        name="couple_tables",
    )(seg_count, in_hbm(coords), in_hbm(weights))


def two_pieces(u):
    high = u.astype(bf16)
    low = u - high.astype(f32)
    return jnp.concatenate([high.astype(f32), low], axis=0).astype(bf16)


def two_small_pieces(u):
    high = u.astype(f8).astype(f32)
    return jnp.concatenate([high, u - high, jnp.zeros((16, u.shape[1]), f32)], axis=0).astype(f8)


def times(pieces, table):
    both = lax.dot_general(pieces, table, (((1,), (0,)), ((), ())), preferred_element_type=f32)
    return both[0:8] + both[8:16]


def times_turned(pieces, table):
    both = lax.dot_general(table, pieces, (((1,), (1,)), ((), ())), preferred_element_type=f32)
    both = jnp.transpose(both)
    return both[0:8] + both[8:16]


COUPLE_BLOCK = 16
SLOTS = 4


def couple_kernel(
    slot_ref, row_ref, high_ref, rest_ref, field_ref, arrived_ref,
    gap_ref, back_ref, highs, rests, held, held_small, field_here, gap_here, sems, field_sem, gap_sem,
):
    count = PAIRS // COUPLE_BLOCK

    def copies(block):
        room = lax.rem(block, SLOTS)
        here = pl.ds(block * COUPLE_BLOCK, COUPLE_BLOCK)
        return (
            pltpu.make_async_copy(high_ref.at[here], highs.at[room], sems.at[0, room]),
            pltpu.make_async_copy(rest_ref.at[here], rests.at[room], sems.at[1, room]),
        )

    def start(block):
        for copy in copies(block):
            copy.start()

    def wait(block):
        for copy in copies(block):
            copy.wait()

    empty = jnp.zeros((5, NODES), f32)

    def pull(block, p):
        room = lax.rem(block, SLOTS)
        pair = block * COUPLE_BLOCK + p
        both = arrived_ref[pl.ds(slot_ref[pair] * PARTS, PARTS), :]
        u = jnp.concatenate([both[0:3], both[3:6]], axis=1)
        u = jnp.concatenate([u, empty], axis=0)
        pulled = times(two_pieces(u), highs[room, p])
        pulled = pulled + times(two_small_pieces(u), rests[room, p]) * (1.0 / REST_SCALE)
        r = row_ref[pair]
        lines = [field_here[c, pl.ds(r, 1), :] for c in range(3)]
        gap = jnp.concatenate(lines + [empty], axis=0) - pulled
        for c in range(3):
            gap_here[c, pl.ds(pair, 1), :] = gap[c : c + 1]
        half = PENALTY * gap
        held[p] = two_pieces(half)
        held_small[p] = two_small_pieces(half)

    def push(block, p):
        room = lax.rem(block, SLOTS)
        back = times_turned(held[p], highs[room, p])
        back = back + times_turned(held_small[p], rests[room, p]) * (1.0 / REST_SCALE)
        back_ref[pl.ds(slot_ref[block * COUPLE_BLOCK + p] * PARTS, PARTS), :] = jnp.concatenate(
            [back[0:3, 0:128], back[0:3, 128:256]], axis=0
        )

    start(0)
    field = pltpu.make_async_copy(field_ref.at[0:3], field_here, field_sem)
    field.start()
    start(1)
    back_ref[...] = jnp.zeros_like(back_ref)
    wait(0)
    start(2)
    field.wait()
    for p in range(COUPLE_BLOCK):
        pull(0, p)

    def one(block, carry):
        wait(block)

        @pl.when(block + SLOTS - 2 < count)
        def _():
            start(block + SLOTS - 2)

        for p in range(COUPLE_BLOCK):
            push(block - 1, p)
            pull(block, p)
        return carry

    lax.fori_loop(1, count, one, 0)
    gaps = pltpu.make_async_copy(gap_here, gap_ref, gap_sem)
    gaps.start()
    for p in range(COUPLE_BLOCK):
        push(count - 1, p)
    gaps.wait()


def couple(slot, slave_row, turned, field, arrived):
    flat = pl.BlockSpec((SLOT_ROWS, 128), lambda *_: (0, 0))
    anywhere = pl.BlockSpec(memory_space=pl.ANY)
    return pl.pallas_call(
        couple_kernel,
        grid_spec=pltpu.PrefetchScalarGridSpec(
            num_scalar_prefetch=2,
            grid=(1,),
            in_specs=[anywhere, anywhere, anywhere, vmem()],
            out_specs=[anywhere, flat],
            scratch_shapes=[
                pltpu.VMEM((SLOTS, COUPLE_BLOCK, NODES, NODES), bf16),
                pltpu.VMEM((SLOTS, COUPLE_BLOCK, NODES, NODES), f8),
                pltpu.VMEM((COUPLE_BLOCK, 16, NODES), bf16),
                pltpu.VMEM((COUPLE_BLOCK, 32, NODES), f8),
                pltpu.VMEM((3, ROWS, NODES), f32),
                pltpu.VMEM((3, PAIRS, NODES), f32),
                pltpu.SemaphoreType.DMA((2, SLOTS)),
                pltpu.SemaphoreType.DMA,
                pltpu.SemaphoreType.DMA,
            ],
        ),
        out_shape=[
            pltpu.HBM((3, PAIRS, NODES), f32),
            pltpu.HBM((SLOT_ROWS, 128), f32),
        ],
        compiler_params=params(),
        name="couple",
    )(slot, slave_row, *turned, in_hbm(field), in_vmem(arrived))


def gathered(hits, lines):
    high = lines.astype(bf16)
    low = (lines - high.astype(f32)).astype(bf16)
    dims = (((1,), (0,)), ((), ()))
    return lax.dot_general(hits, high, dims, preferred_element_type=f32) + lax.dot_general(
        hits, low, dims, preferred_element_type=f32
    )


def inside():
    slab, face = lax.axis_index("slab"), lax.axis_index("face")
    there = [slab > 0, slab < lax.axis_size("slab") - 1, face > 0, face < lax.axis_size("face") - 1]
    return [jnp.where(neighbour, 1.0, 0.0) for neighbour in there]


def turned_sides(within, left_ref, right_ref):
    count = left_ref.shape[0]
    pad = jnp.zeros((8 - count, ROWS), f32)
    left, right = left_ref[...] * within[2], right_ref[...] * within[3]
    x = jnp.concatenate([left, pad, right, pad], axis=0)
    high = x.astype(bf16).astype(f32)
    rest = x - high
    middle = rest.astype(bf16).astype(f32)
    pieces = jnp.concatenate([high, middle, rest - middle, jnp.zeros((80, ROWS), f32)], axis=0)
    return jnp.transpose(pieces).astype(bf16)


def inner(u):
    row = lax.broadcasted_iota(jnp.int32, (ROWS, NODES), 0)
    col = lax.broadcasted_iota(jnp.int32, (ROWS, NODES), 1)
    up = jnp.where(row == 0, 0.0, pltpu.roll(u, 1, 0))
    down = jnp.where(row == ROWS - 1, 0.0, pltpu.roll(u, ROWS - 1, 0))
    west = jnp.where(col == 0, 0.0, pltpu.roll(u, 1, 1))
    east = jnp.where(col == NODES - 1, 0.0, pltpu.roll(u, NODES - 1, 1))
    return (down + up) + (east + west)


def rim(within, above_ref, below_ref, sides, c):
    row = lax.broadcasted_iota(jnp.int32, (ROWS, NODES), 0)
    piece = lax.broadcasted_iota(jnp.int32, (128, NODES), 0) & 15
    place = lax.broadcasted_iota(jnp.int32, (128, NODES), 1)
    pick = ((piece == c) & (place == 0)) | ((piece == 8 + c) & (place == NODES - 1))
    pick = jnp.where(pick, 1.0, 0.0).astype(bf16)
    beside = lax.dot_general(sides, pick, (((1,), (0,)), ((), ())), preferred_element_type=f32)
    above = above_ref[c : c + 1, :] * within[0]
    below = below_ref[c : c + 1, :] * within[1]
    return beside + jnp.where(row == 0, above, jnp.where(row == ROWS - 1, below, 0.0))


def swept(u, right, gain, around):
    return (1.0 - RELAX) * u + gain * (right + around)


def put_edges(c, u, edges):
    top, bottom, left, right = edges
    top[c : c + 1, :] = u[0:1]
    bottom[c : c + 1, :] = u[ROWS - 1 : ROWS]
    left[c : c + 1, :] = jnp.transpose(u[:, 0:128])[0:1]
    right[c : c + 1, :] = jnp.transpose(u[:, 128:256])[127:128]


def early_sweep_kernel(row_ref, gap_ref, u_ref, load_ref, stiff_ref, right_out, first_out, gain_out):
    row = lax.broadcasted_iota(jnp.int32, (ROWS, PAIRS), 0)
    hits = jnp.where(row == row_ref[...], 1.0, 0.0).astype(bf16)
    gain = RELAX / (4.0 + stiff_ref[...])
    gain_out[...] = gain
    for c in range(6):
        right = load_ref[c]
        if c < 3:
            right = right - PENALTY * gathered(hits, gap_ref[c])
        right_out[c] = right
        first_out[c] = swept(u_ref[c], right, gain, inner(u_ref[c]))


def early_sweep(slave_row, gap, displacement, load, stiffness):
    whole = pl.BlockSpec((6, ROWS, NODES), lambda i: (0, 0, 0))
    plane = pl.BlockSpec((ROWS, NODES), lambda i: (0, 0))
    field = pltpu.HBM((6, ROWS, NODES), f32)
    return pl.pallas_call(
        early_sweep_kernel,
        grid=(1,),
        out_shape=[field, field, pltpu.HBM((ROWS, NODES), f32)],
        in_specs=[
            vmem(), pl.BlockSpec((3, PAIRS, NODES), lambda i: (0, 0, 0)), whole, whole, plane
        ],
        out_specs=[whole, whole, plane],
        compiler_params=params(),
        name="early_sweep",
    )(slave_row, in_hbm(gap), in_hbm(displacement), in_hbm(load), in_hbm(stiffness))


def edges_kernel(u_ref, *edges):
    for c in range(6):
        put_edges(c, u_ref[c], edges)


def first_edges(displacement):
    return pl.pallas_call(
        edges_kernel,
        out_shape=[jax.ShapeDtypeStruct((6, 256), f32)] * 4,
        in_specs=[vmem()],
        out_specs=[vmem()] * 4,
        compiler_params=params(),
        name="first_edges",
    )(displacement)


def master_sweep_kernel(
    asked_ref, incoming_ref, first_ref, gain_ref, ha, hb, hl, hr,
    u_out, added_out, *refs
):
    edges, first, gain_here, sems = refs[:4], *refs[4:]
    within = inside()
    arrivals = [
        pltpu.make_async_copy(first_ref.at[c], first.at[c], sems.at[c]) for c in range(6)
    ]
    arrivals.append(pltpu.make_async_copy(gain_ref, gain_here, sems.at[6]))
    for k in (6, 3, 4, 5, 0, 1, 2):
        arrivals[k].start()
    asked = jnp.transpose(asked_ref[...].reshape(DEVICES, 128))
    row = lax.broadcasted_iota(jnp.int32, (ROWS, DEVICES), 0)
    hits = jnp.concatenate(
        [jnp.where(row == asked[k : k + 1], 1.0, 0.0) for k in range(CAP)], axis=1
    ).astype(bf16)

    def lines(part):
        return jnp.concatenate(
            [
                incoming_ref[pl.ds(k * PARTS + part, DEVICES, stride=CAP * PARTS), :]
                for k in range(CAP)
            ],
            axis=0,
        )

    sides = turned_sides(within, hl, hr)
    for c in (3, 4, 5, 0, 1, 2):
        more = rim(within, ha, hb, sides, c)
        if c >= 3:
            added = gathered(hits, jnp.concatenate([lines(c - 3), lines(c)], axis=1))
            added_out[c - 3] = added
            more = more + added
        if c == 3:
            arrivals[6].wait()
        arrivals[c].wait()
        u = first[c] + gain_here[...] * more
        u_out[c] = u
        put_edges(c, u, edges)


def master_sweep(asked, incoming, first, gain, halos):
    lines = jax.ShapeDtypeStruct((6, 256), f32)
    return pl.pallas_call(
        master_sweep_kernel,
        out_shape=[jax.ShapeDtypeStruct((n, ROWS, NODES), f32) for n in (6, 3)] + [lines] * 4,
        in_specs=[
            vmem(),
            vmem(),
            pl.BlockSpec(memory_space=pl.ANY),
            pl.BlockSpec(memory_space=pl.ANY),
        ]
        + [vmem()] * 4,
        out_specs=[vmem()] * 6,
        scratch_shapes=[
            pltpu.VMEM((6, ROWS, NODES), f32),
            pltpu.VMEM((ROWS, NODES), f32),
            pltpu.SemaphoreType.DMA((7,)),
        ],
        compiler_params=params(),
        name="master_sweep",
    )(asked, in_vmem(incoming), in_hbm(first), in_hbm(gain), *halos)


def last_sweep_kernel(
    u_ref, right_ref, added_ref, gain_ref, ha, hb, hl, hr, out_ref, done, sems
):
    copies = []
    within = inside()
    gain = gain_ref[...]
    sides = turned_sides(within, hl, hr)
    for c in range(6):
        right = right_ref[c] if c < 3 else right_ref[c] + added_ref[c - 3]
        around = inner(u_ref[c]) + rim(within, ha, hb, sides, c)
        done[c] = swept(u_ref[c], right, gain, around)
        copies.append(pltpu.make_async_copy(done.at[c], out_ref.at[c], sems.at[c]))
        copies[-1].start()
    for copy in copies:
        copy.wait()


def last_sweep(u, right, added, gain, halos):
    return pl.pallas_call(
        last_sweep_kernel,
        out_shape=jax.ShapeDtypeStruct((6, ROWS, NODES), f32),
        in_specs=[vmem()] * 8,
        out_specs=pl.BlockSpec(memory_space=pl.ANY),
        scratch_shapes=[pltpu.VMEM((6, ROWS, NODES), f32), pltpu.SemaphoreType.DMA((6,))],
        compiler_params=params(),
        name="last_sweep",
    )(u, right, added, gain, *halos)


def exchange(top, bottom, left, right):
    slabs, faces = lax.axis_size("slab"), lax.axis_size("face")
    onward = lambda n: [(i, (i + 1) % n) for i in range(n)]
    back = lambda n: [((i + 1) % n, i) for i in range(n)]
    return (
        lax.ppermute(bottom, "slab", onward(slabs)),
        lax.ppermute(top, "slab", back(slabs)),
        lax.ppermute(right, "face", onward(faces)),
        lax.ppermute(left, "face", back(faces)),
    )


def all_to_all(x):
    return lax.all_to_all(x, AXES, split_axis=0, concat_axis=0, tiled=True)


def body(
    displacement,
    load,
    stiffness,
    slave_row,
    master_dev,
    master_row,
    seg_count,
    quad_coords,
    quad_weights,
):
    request, slot = slots(master_dev.reshape(1, PAIRS), master_row.reshape(1, PAIRS))
    slot = slot.reshape(PAIRS)
    asked = all_to_all(request)
    first_halos = exchange(*first_edges(displacement))
    turned = couple_tables(seg_count, quad_coords, quad_weights)
    served = serve(asked.reshape(DEVICES * 128), displacement)
    arrived = all_to_all(served).reshape(SLOT_ROWS, 128)
    gap, outgoing = couple(slot, slave_row, turned, displacement, arrived)
    incoming = all_to_all(outgoing.reshape(DEVICES, CAP * PARTS, 128)).reshape(SLOT_ROWS, 128)
    right, first, gain = early_sweep(
        slave_row.reshape(1, PAIRS), gap, displacement, load, stiffness
    )
    u, added, *edges = master_sweep(asked, incoming, first, gain, first_halos)
    relaxed = last_sweep(u, right, added, gain, exchange(*edges))
    return relaxed, gap.transpose(1, 0, 2)


def solution(mesh):
    pairs = P(AXES)
    field = P(None, "slab", "face")
    return jax.shard_map(
        body,
        mesh=mesh,
        in_specs=(
            field,
            field,
            P("slab", "face"),
            pairs,
            P(AXES, None),
            pairs,
            pairs,
            P(AXES, None, None),
            P(AXES, None),
        ),
        out_specs=(field, P(AXES, None, None)),
        check_vma=False,
    )
```
